512 devices in a mesh: dx: 16 (over y, x), dy: 32 (over z, core).
Axes of the slice: x: 4, y: 4, z: 16, core: 2. Of those that a mesh axis runs over, the one named last changes fastest.
Arguments:
- audio: bfloat16 [32, 128, 2570], P('dy', 'dx'), may hold values from -6 to 6
- counts: int32 [32, 16], P('dy', 'dx'), may hold values from 1 to 8, 64 in all within a row
- cotangent: bfloat16 [32, 64, 256, 512], P('dy', 'dx'), may hold values from -6 to 6
- conv_first: bfloat16 [10, 512], replicated, may hold values from -2 to 2
- norm_gain: float32 [512], replicated, may hold values from 0.1 to 1.9
- norm_bias: float32 [512], replicated, may hold values from -3 to 3
- conv_second: bfloat16 [1536, 512], replicated, may hold values from -0.15625 to 0.15625
Outputs:
- grad_conv_first: float32 [10, 512], replicated
- grad_norm: float32 [2, 512], replicated
- grad_conv_second: float32 [1536, 512], P('dy')
The draws below stay inside these ranges and needn't reach their ends.
Inputs may be any that keep to these rules, and one draw needn't show every extreme that they name: In each group along dy the counts sum to 64, and some device of each group holds exactly 8 live crops.
All inputs are finite; a program needn't handle non-finite values.
Results may differ from the reference program's by a relative error of at most 0.0051.
Values may be sent and summed in bfloat16 or wider, within the bound.
A program may use at most 128 MiB of HBM per device.

```python
import math
import jax
import jax.numpy as jnp
import numpy as np
from jax import lax

C = 512
RECV = 4
T2 = 256
SLOTS = 8
CROP = 2570
CROPS = 64
GROUPS = 32
PEERS = 16


def block_scale(stream_key, shape, pieces, low, top_value):
    def one(position, shards_of):
        draws = jax.random.uniform(jax.random.fold_in(jax.random.fold_in(stream_key, 6), position), (shards_of,), jnp.float32, low / len(pieces), top_value / len(pieces))
        return jnp.repeat(jnp.exp(draws), shape[position] // shards_of).reshape((-1,) + (1,) * (len(shape) - position - 1))

    loudness = one(*pieces[0])
    for cut in pieces[1:]:
        loudness = loudness * one(*cut)
    return loudness


def split_up(number_of, total, reach, slope):
    loads = [(1 << 20) // math.isqrt(standing ** slope) + 1 for standing in range(2, number_of + 1)]
    rest, given = total - reach - (number_of - 1), [1] * (number_of - 1)
    while rest > 0:
        movable = [i for i in range(number_of - 1) if given[i] < reach]
        whole, left = sum([loads[i] for i in movable]), rest
        for i in movable:
            extra = min(reach - given[i], max(1, left * loads[i] // whole), rest)
            given[i] = given[i] + extra
            rest = rest - extra
    return np.array([reach] + given)


def ragged_sizes(rng, number_of, total, reach, skew):
    if number_of == 2:
        one = jax.random.randint(rng, (), max(1, total - reach), min(reach, total - 1) + 1)
        return jnp.stack([one, total - one])
    lengths = jnp.asarray(split_up(number_of, total, reach, skew), jnp.int32)
    pairs = (number_of - 1) // 2
    giver, receiver = lengths[1:1 + 2 * pairs:2], lengths[2:2 + 2 * pairs:2]
    room = jnp.minimum(giver - 1, reach - receiver)
    passed = jax.random.randint(jax.random.fold_in(rng, 1), (pairs,), 0, 1 << 20) % (room + 1)
    lengths = lengths.at[1:1 + 2 * pairs:2].set(giver - passed).at[2:2 + 2 * pairs:2].set(receiver + passed)
    return lengths[jax.random.permutation(jax.random.fold_in(rng, 2), number_of)]


def scatter_about(stream_key, shape, deviation, most, split=(), kind=jnp.bfloat16):
    gain = block_scale(stream_key, shape, split, -0.22, 0.18) if split else 1.0
    entries = jax.random.normal(stream_key, shape, jnp.float32) * deviation * gain
    return jnp.minimum(jnp.maximum(entries, -most), most).astype(kind)


def setup_inputs(seed: int = 0) -> dict:
    key_list = jax.random.split(jax.random.key(seed), 8)
    return {
        "audio": scatter_about(key_list[0], (GROUPS, PEERS * SLOTS, CROP), 1.0, 6.0, ((0, 32), (1, 16))),
        "counts": jax.vmap(lambda own: ragged_sizes(own, PEERS, CROPS, SLOTS, 2))(jax.random.split(key_list[1], GROUPS)).reshape((GROUPS, PEERS)).astype(jnp.int32),
        "cotangent": scatter_about(key_list[2], (GROUPS, CROPS, T2, C), 1.0, 6.0, ((0, 32), (1, 16))),
        "conv_first": scatter_about(key_list[3], (10, C), 10 ** -0.5, 2.0),
        "norm_gain": jnp.clip(1.0 + 0.18 * jax.random.normal(key_list[4], (C,), jnp.float32), 0.1, 1.9),
        "norm_bias": scatter_about(key_list[5], (C,), 0.5, 3.0, (), jnp.float32),
        "conv_second": scatter_about(key_list[6], (3 * C, C), (3 * C) ** -0.5, 0.15625),
    }


def gelu_cdf(value):
    return 0.5 * (1.0 + lax.erf(value * 0.7071067811865476))

def gelu_slope(value):
    return gelu_cdf(value) + value * jnp.exp(-0.5 * value * value) * 0.3989422804014327

def forward_backward(crop_waves, cot_rows, conv_first, norm_gain, norm_bias, conv_second, loss_scale):
    batch_size = crop_waves.shape[0]
    frames = cot_rows.shape[1]
    first_len = 2 * frames + 1
    channels = conv_second.shape[1]
    early_taps = crop_waves[:, :5 * first_len].reshape(batch_size, first_len, 5)
    late_taps = crop_waves[:, 5:5 * first_len + 5].reshape(batch_size, first_len, 5)
    patches = jnp.concatenate([early_taps, late_taps], axis=2).reshape(batch_size * first_len, 10)
    pre_norm = jnp.dot(patches, conv_first, preferred_element_type=jnp.float32).reshape(batch_size, first_len, channels)
    centre = pre_norm - lax.optimization_barrier(jnp.mean(pre_norm, axis=1, keepdims=True))
    inv_std = lax.rsqrt(lax.optimization_barrier(jnp.mean(centre * centre, axis=1, keepdims=True)) + 1e-05)
    normed = centre * inv_std
    shifted = normed * norm_gain + norm_bias
    hidden = (shifted * gelu_cdf(shifted)).astype(jnp.bfloat16)
    two_taps = hidden[:, :2 * frames].reshape(batch_size, frames, 2 * channels)
    third_tap = hidden[:, 2::2]
    second_rows = jnp.concatenate([two_taps, third_tap], axis=2).reshape(batch_size * frames, 3 * channels)
    pre_act = jnp.dot(second_rows, conv_second, preferred_element_type=jnp.float32)
    grad_rows = (loss_scale * cot_rows.reshape(batch_size * frames, channels).astype(jnp.float32) * gelu_slope(pre_act)).astype(jnp.bfloat16)
    grad_cols = jnp.dot(grad_rows, conv_second.T, preferred_element_type=jnp.float32).reshape(batch_size, frames, 3 * channels)
    first_taps = grad_cols[:, :, :2 * channels].reshape(batch_size, 2 * frames, channels)
    late_tap = jnp.stack([grad_cols[:, :, 2 * channels:], jnp.zeros((batch_size, frames, channels), jnp.float32)], axis=2).reshape(batch_size, 2 * frames, channels)
    grad_hidden = jnp.concatenate([first_taps, jnp.zeros((batch_size, 1, channels), jnp.float32)], axis=1)
    grad_hidden = grad_hidden + jnp.concatenate([jnp.zeros((batch_size, 2, channels), jnp.float32), late_tap[:, :2 * frames - 1]], axis=1)
    grad_shift = grad_hidden * gelu_slope(shifted)
    gain_grad = lax.optimization_barrier(jnp.sum(grad_shift * normed, axis=(0, 1)))
    shift_grad = lax.optimization_barrier(jnp.sum(grad_shift, axis=(0, 1)))
    grad_scaled = grad_shift * norm_gain
    grad_pre = inv_std * (grad_scaled - lax.optimization_barrier(jnp.mean(grad_scaled, axis=1, keepdims=True)) - normed * lax.optimization_barrier(jnp.mean(grad_scaled * normed, axis=1, keepdims=True)))
    grad_pre = grad_pre.astype(jnp.bfloat16).reshape(batch_size * first_len, channels)
    grad_first = jnp.dot(patches.T, grad_pre, preferred_element_type=jnp.float32)
    return (second_rows, grad_rows, grad_first, jnp.stack([gain_grad, shift_grad]))

def reference(audio, counts, cotangent, conv_first, norm_gain, norm_bias, conv_second):
    loss_scale = 1.0 / math.sqrt(GROUPS * CROPS * T2)

    def group_step(totals, inputs):
        waves_all, row_counts, row_cot = inputs
        starts = jnp.cumsum(row_counts, dtype=jnp.int32) - row_counts
        positions = jnp.arange(CROPS, dtype=jnp.int32)
        wanted = positions % RECV * PEERS + positions // RECV
        holder = lax.optimization_barrier(jnp.sum((starts[None, :] <= wanted[:, None]).astype(jnp.int32), axis=1, dtype=jnp.int32)) - 1
        offset = wanted - starts[holder]
        crop_waves = jnp.take(waves_all, holder * SLOTS + offset, axis=0)
        second_rows, grad_rows, grad_first, grad_gains = forward_backward(crop_waves, row_cot, conv_first, norm_gain, norm_bias, conv_second, loss_scale)
        grad_second = jnp.dot(second_rows.T, grad_rows, preferred_element_type=jnp.float32)
        updated = (totals[0] + grad_first, totals[1] + grad_gains, totals[2] + grad_second)
        return (updated, None)
    start_sums = (jnp.zeros((10, C), jnp.float32), jnp.zeros((2, C), jnp.float32), jnp.zeros((3 * C, C), jnp.float32))
    totals, unused = lax.scan(group_step, start_sums, (audio, counts, cotangent))
    return (totals[0], totals[1], totals[2])
```

```python
import functools
import math

import jax
import jax.numpy as jnp
from jax import lax
from jax.experimental import pallas as pl
from jax.experimental.pallas import tpu as pltpu
from jax.sharding import PartitionSpec as P

F32 = jnp.float32
BF16 = jnp.bfloat16
MESH = pl.DeviceIdType.MESH
SIDE = 4
TN = (((0,), (0,)), ((), ()))
NT = (((1,), (1,)), ((), ()))
NN = (((1,), (0,)), ((), ()))
LOG2E = 1.4426950408889634


def dot(a, b, dims=NN):
    return lax.dot_general(a, b, dims, preferred_element_type=F32)


def pieces(value):
    high = value.astype(BF16)
    rest = value - high.astype(F32)
    mid = rest.astype(BF16)
    low = (rest - mid.astype(F32)).astype(BF16)
    return high, mid, low


def gelu_parts(value):
    cdf = 0.5 * lax.erf(value * 0.7071067811865476) + 0.5
    slope = cdf + value * (jnp.exp2(value * value * (-0.5 * LOG2E)) * 0.3989422804014327)
    return cdf, slope


def rows_of(shape):
    return lax.broadcasted_iota(jnp.int32, shape, 0)


def cols_of(shape):
    return lax.broadcasted_iota(jnp.int32, shape, 1)


def kernel(
    planes, depth, scale,
    audio_hbm, counts_ref, cot_hbm, w1_hbm, gain_hbm, bias_hbm, w2_hbm,
    first_out, norm_out, second_out,
    audio, cot, w1, gain_ref, bias_ref, w2, load_sem,
    perm, zbuf, cnt_all, crop_send, crop_recv, xf, xp, weo, wpad, waug, gw, stat, colsum,
    hid, grows, slope_e, slope_o, slope_t, hshift, dshift,
    half_sum, pair_send, pair_recv,
    x_send, x_recv, y_send, y_recv, xa, ya, x2_send, x2_recv, y2_send, y2_recv,
    part, z_send, z_recv, full, gathered,
    acc_e, acc_o, acc_t, small, s_send, s_recv, u_val, u_recv, v_val, v_recv,
    cnt_ss, cnt_rs, crop_ss, crop_rs, pair_ss, pair_rs, plane_ss, plane_rs,
    z_ss, z_rs, d_ss, d_rs, s1_ss, s1_rs, s2_ss, s2_rs, s3_ss, s3_rs,
):
    me = lax.axis_index("dx")
    dy = lax.axis_index("dy")
    core = lax.rem(dy, 2)
    z = dy // 2
    px = lax.rem(me, SIDE)
    py = me // SIDE
    zhalf = depth // 2
    frames = cot_hbm.shape[2]
    channels = w2_hbm.shape[1]
    rows_all = w2_hbm.shape[0]
    half_rows = rows_all // 2
    rz = rows_all // depth
    rx = rz // SIDE
    hz = zhalf // 2
    hrows = half_rows // 2
    total_frames = 2 * frames + 1
    crops = cot_hbm.shape[1]

    def send(src, dst, ss, rs, where):
        return pltpu.make_async_remote_copy(
            src_ref=src, dst_ref=dst, send_sem=ss, recv_sem=rs,
            device_id=where, device_id_type=MESH,
        )

    loads = [
        pltpu.make_async_copy(src, dst, load_sem.at[i])
        for i, (src, dst) in enumerate(
            ((audio_hbm, audio), (w1_hbm, w1), (gain_hbm, gain_ref), (bias_hbm, bias_ref),
             (w2_hbm, w2), (cot_hbm, cot))
        )
    ]
    for load in loads:
        load.start()

    barrier = pltpu.get_barrier_semaphore()

    @pl.loop(0, planes)
    def _(p):
        @pl.when(p != me)
        def _():
            pl.semaphore_signal(barrier, inc=1, device_id=(p, dy), device_id_type=MESH)

        pl.semaphore_signal(barrier, inc=1, device_id=(p, 2 * z + 1 - core), device_id_type=MESH)

    @pl.loop(0, depth)
    def _(k):
        @pl.when(k != z)
        def _():
            pl.semaphore_signal(barrier, inc=1, device_id=(me, 2 * k + core), device_id_type=MESH)

    lane = cols_of((1, 640))
    sample = 10 * (lane % 64) + 2 * (lane // 128) + (lane % 128) // 64
    for i in range(5):
        block = rows_of((128, 640)) + 128 * i
        perm[pl.ds(128 * i, 128), :] = jnp.where(block == sample, 1.0, 0.0).astype(BF16)
    cnt_all[me] = jnp.full((1, 128), counts_ref[0, 0], jnp.int32)

    loads[0].wait()
    blocks = jnp.concatenate(
        [audio[0, :, 640 * i : 640 * i + 640].astype(F32) for i in range(4)], axis=0
    ).astype(BF16)
    sorted_blocks = dot(blocks, perm[...])
    eye = jnp.where(rows_of((10, 256)) == cols_of((10, 256)), 1.0, 0.0).astype(BF16)
    tails = dot(audio[0, :, 2560:2570], eye)
    low_lane = cols_of((8, 128)) < 64
    last_lane = cols_of((8, 256)) == 255
    for m in range(10):
        g = m // 2
        parts = []
        for half in range(2):
            a = sorted_blocks[16 * half : 16 * half + 8, 128 * g : 128 * g + 128]
            b = sorted_blocks[16 * half + 8 : 16 * half + 16, 128 * g : 128 * g + 128]
            if m % 2 == 0:
                parts.append(jnp.where(low_lane, a, pltpu.roll(b, 64, 1)))
            else:
                parts.append(jnp.where(low_lane, pltpu.roll(a, 64, 1), b))
        row = jnp.concatenate(parts, axis=1)
        zbuf[:, m, :] = row
        if m < 5:
            zbuf[:, 11 + m, :] = jnp.where(last_lane, tails[:, m : m + 1], pltpu.roll(row, 255, 1))
    zbuf[:, 10, :] = tails
    slot_rows = zbuf[...].reshape(128, 256).astype(BF16)

    waug[...] = jnp.zeros_like(waug)
    loads[1].wait()
    loads[2].wait()
    loads[3].wait()
    w1v = w1[...].astype(F32)
    weo[...] = jnp.zeros_like(weo)
    weo[0:10, 0:channels] = w1v
    weo[5:10, channels:] = w1v[0:5]
    weo[11:16, channels:] = w1v[5:10]
    wpad[...] = jnp.zeros_like(wpad)
    wpad[0:10, :] = w1v

    pl.semaphore_wait(barrier, 2 * planes - 1 + depth - 1)

    @pl.loop(1, planes)
    def _(k):
        to = lax.rem(me + k, planes)
        send(cnt_all.at[me], cnt_all.at[me], cnt_ss.at[k], cnt_rs.at[k], (to, dy)).start()

    @pl.loop(1, planes)
    def _(k):
        frm = lax.rem(me - k + planes, planes)
        send(cnt_all.at[me], cnt_all.at[frm], cnt_ss.at[k], cnt_rs.at[k], (frm, dy)).wait()

    count_rows = cnt_all[...].reshape(planes, 128)
    who = rows_of((planes, 128))
    start_me = jnp.sum(jnp.where(who < me, count_rows, 0), axis=0, keepdims=True)
    count_me = jnp.sum(jnp.where(who == me, count_rows, 0), axis=0, keepdims=True)
    shape = (16 * planes, 128)
    rr, cc = rows_of(shape), cols_of(shape)
    slot = cc // 16
    pick = (rr % 16 == cc % 16) & (slot < count_me) & ((start_me + slot) % planes == rr // 16)
    routed = dot(jnp.where(pick, 1.0, 0.0).astype(BF16), slot_rows).astype(BF16)
    crop_send[...] = routed.reshape(planes, 16, 256)

    @pl.loop(1, planes)
    def _(k):
        to = lax.rem(me + k, planes)
        send(crop_send.at[to], crop_recv.at[me], crop_ss.at[k], crop_rs.at[k], (to, dy)).start()

    crop_recv[me] = crop_send[me]
    wide = jnp.concatenate([count_rows, count_rows], axis=1)
    who2, col2 = rows_of((planes, 256)), cols_of((planes, 256)) // 16
    start_col = jnp.sum(jnp.where(who2 < col2, wide, 0), axis=0, keepdims=True)
    count_col = jnp.sum(jnp.where(who2 == col2, wide, 0), axis=0, keepdims=True)
    shape = (16 * crops, 256)
    rr, cc = rows_of(shape), cols_of(shape)
    order = (rr // 16) * planes + me
    pick = (rr % 16 == cc % 16) & (start_col <= order) & (order < start_col + count_col)
    pick = jnp.where(pick, 1.0, 0.0).astype(BF16)

    @pl.loop(1, planes)
    def _(k):
        frm = lax.rem(me - k + planes, planes)
        send(crop_send.at[frm], crop_recv.at[frm], crop_ss.at[k], crop_rs.at[k], (frm, dy)).wait()

    mine = dot(pick, crop_recv[...].reshape(16 * planes, 256))
    xf[...] = mine
    xp_all = jnp.where(rows_of((16 * crops, 256)) % 16 == 10, 1.0, mine)
    xp[...] = xp_all.astype(BF16)
    xt = jnp.concatenate([xp_all] * 3, axis=0).T.astype(BF16)

    tail_rows = jnp.concatenate(
        [xf[16 * r + 10 : 16 * r + 11, 0:128] for r in range(crops)]
        + [jnp.zeros((8 - crops, 128), F32)], axis=0)
    tail_pre = dot(tail_rows.astype(BF16), wpad[...].astype(BF16))
    gain = gain_ref[...].reshape(1, channels)
    bias = bias_ref[...].reshape(1, channels)
    we, wo = weo[:, 0:channels], weo[:, channels:]
    weo16 = weo[...].astype(BF16)
    row16 = rows_of((16, channels))
    for r in range(crops):
        x16 = xp[16 * r : 16 * r + 16, :]
        gram = dot(x16, x16, NT)
        g1, g2, g3 = pieces(gram)
        gwv = dot(g1, weo16) + dot(g2, weo16) + dot(g3, weo16)
        gw[r] = gwv
        colsum[r] = jnp.broadcast_to(gram[:, 10:11], (16, 128))
        pre_t = tail_pre[r : r + 1]
        gwe, gwo = gwv[:, 0:channels], gwv[:, channels:]
        mu = (gwe[10:11] + gwo[10:11] + pre_t) * (1.0 / total_frames)
        square = jnp.sum(we * gwe + wo * gwo, axis=0, keepdims=True) + pre_t * pre_t
        var = jnp.maximum(square * (1.0 / total_frames) - mu * mu, 0.0)
        inv = lax.rsqrt(var + 1e-5)
        mul = inv * gain
        add = bias - mu * mul
        stat[r, 0:1] = mu
        stat[r, 1:2] = inv
        stat[r, 2:3] = mul
        stat[r, 3:4] = pre_t
        stat[r, 4:5] = pre_t * mul + add
        for side, w in ((0, we), (1, wo)):
            scaled = jnp.where(row16 == 10, add, w * mul)
            for i, piece in enumerate(pieces(scaled)):
                waug[r, 64 * i + 16 * r : 64 * i + 16 * r + 16,
                     side * channels : (side + 1) * channels] = piece

    loads[4].wait()
    loads[5].wait()
    quarter = channels // 2
    xt_parts = [xt[128 * i : 128 * i + 128] for i in range(frames // 128)]

    @pl.loop(0, crops)
    def _(r):
        base = pl.multiple_of(r * frames, frames)
        tail = stat[r, 4:5]
        cdf, slope = gelu_parts(tail)
        hshift[frames : frames + 1, :] = tail * cdf
        slope_t[r] = slope
        for n in range(4):
            for i in range(frames // 128):
                value = dot(xt_parts[i], waug[r, :, n * quarter : (n + 1) * quarter])
                cdf, slope = gelu_parts(value)
                value = value * cdf
                lo = (n % 2) * quarter
                if n < 2:
                    slope_e[r, 128 * i : 128 * i + 128, lo : lo + quarter] = slope
                    hshift[128 * i : 128 * i + 128, lo : lo + quarter] = value
                    hid[0, pl.ds(base + 128 * i, 128), lo : lo + quarter] = value.astype(BF16)
                else:
                    slope_o[r, 128 * i : 128 * i + 128, lo : lo + quarter] = slope
                    at = 512 if n == 2 else 0
                    hid[n - 2, pl.ds(base + 128 * i, 128), at : at + quarter] = value.astype(BF16)
        hid[1, pl.ds(base, frames), quarter:] = hshift[1 : frames + 1, :].astype(BF16)
        for n in range(2):
            cols = slice(n * quarter, (n + 1) * quarter)
            pre = dot(hid[0, pl.ds(base, frames), :], w2[0:half_rows, cols])
            pre = pre + dot(hid[1, pl.ds(base, frames), :], w2[half_rows:, cols])
            slope = gelu_parts(pre)[1]
            grad = (scale * cot[0, r, :, cols].astype(F32)) * slope
            grows[pl.ds(base, frames), cols] = grad.astype(BF16)

    pair = (me, 2 * z + 1 - core)
    for h in range(2):
        theirs = dot(hid[1 - core, :, h * hrows : (h + 1) * hrows], grows[...], TN)
        pair_send[h] = theirs.astype(BF16)
        send(pair_send.at[h], pair_recv.at[h], pair_ss.at[h], pair_rs.at[h], pair).start()
    for h in range(2):
        half_sum[h] = dot(hid[core, :, h * hrows : (h + 1) * hrows], grows[...], TN)

    acc_e[...] = jnp.zeros_like(acc_e)
    acc_o[...] = jnp.zeros_like(acc_o)
    acc_t[...] = jnp.zeros_like(acc_t)
    small[...] = jnp.zeros_like(small)
    dshift[0:8, :] = jnp.zeros((8, channels), F32)

    def backward(r):
        base = pl.multiple_of(r * frames, frames)
        grad = grows[pl.ds(base, frames), :]
        x16 = xp[pl.ds(pl.multiple_of(16 * r, 16), 16), :]
        shift_o = dot(grad, w2[channels : 2 * channels, :], NT) * slope_o[r]
        p_o = dot(x16, shift_o.astype(BF16))
        dshift[8 : 8 + frames, :] = dot(grad, w2[2 * channels :, :], NT)
        shift_e = dot(grad, w2[0:channels, :], NT) + dshift[7 : 7 + frames, :]
        p_e = dot(x16, (shift_e * slope_e[r]).astype(BF16))
        shift_t = dshift[7 + frames : 8 + frames, :] * slope_t[r]
        mu, inv, mul, pre_t = stat[r, 0:1], stat[r, 1:2], stat[r, 2:3], stat[r, 3:4]
        total = p_e[10:11] + p_o[10:11] + shift_t
        with_pre = jnp.sum(weo[:, 0:channels] * p_e + weo[:, channels:] * p_o, axis=0, keepdims=True)
        with_norm = inv * (with_pre + pre_t * shift_t - mu * total)
        small[10:11, :] = small[10:11, :] + with_norm
        small[11:12, :] = small[11:12, :] + total
        mean_g = total * (1.0 / total_frames)
        mean_n = with_norm * (1.0 / total_frames) * inv
        sums = jnp.concatenate([colsum[r]] * (channels // 128), axis=1)
        base_part = mean_g * sums
        acc_e[...] += mul * (p_e - base_part - mean_n * (gw[r, :, 0:channels] - mu * sums))
        acc_o[...] += mul * (p_o - base_part - mean_n * (gw[r, :, channels:] - mu * sums))
        acc_t[pl.ds(r, 1), :] = mul * (shift_t - mean_g - mean_n * (pre_t - mu))

    @pl.loop(0, crops // 2)
    def _(r):
        backward(r)

    def peer_x(k):
        return lax.rem(px + k, SIDE)

    def peer_y(k):
        return lax.rem(py + k, SIDE)

    def x_rows(ref, x):
        return jnp.concatenate(
            [ref[pl.ds(pl.multiple_of(i * rz + x * rx, 8), rx), :] for i in range(hz)], axis=0)

    def y_lanes(ref, y):
        return ref[:, pl.ds(pl.multiple_of(128 * y, 128), 128)]

    def at_x(x):
        return (py * SIDE + x, dy)

    def at_y(y):
        return (y * SIDE + px, dy)

    def pair_wait(h):
        send(pair_send.at[h], pair_recv.at[h], pair_ss.at[h], pair_rs.at[h], pair).wait()
        half_sum[h] = half_sum[h] + pair_recv[h].astype(F32)

    def x_copy(k):
        return send(x_send.at[k], x_recv.at[k], plane_ss.at[k], plane_rs.at[k], at_x(peer_x(k)))

    def y_copy(k):
        return send(y_send.at[k], y_recv.at[k], plane_ss.at[4 + k], plane_rs.at[4 + k], at_y(peer_y(k)))

    def y2_copy(k):
        return send(y2_send.at[k], y2_recv.at[k], plane_ss.at[8 + k], plane_rs.at[8 + k], at_y(peer_y(k)))

    def x2_copy(k):
        return send(x2_send.at[k], x2_recv.at[k], plane_ss.at[12 + k], plane_rs.at[12 + k], at_x(peer_x(k)))

    pair_wait(0)
    for k in range(1, SIDE):
        x_send[k] = x_rows(half_sum.at[0], peer_x(k)).astype(BF16)
        x_copy(k).start()
    pair_wait(1)
    for k in range(1, SIDE):
        y_send[k] = y_lanes(half_sum.at[1], peer_y(k)).astype(BF16)
        y_copy(k).start()

    @pl.loop(crops // 2, crops)
    def _(r):
        backward(r)

    tail_grad = lax.dot_general(
        tail_rows, acc_t[...], TN, preferred_element_type=F32, precision=lax.Precision.HIGHEST)
    small[0:10, :] = acc_e[0:10, :] + tail_grad[0:10, :]
    small[0:5, :] = small[0:5, :] + acc_o[5:10, :]
    small[5:10, :] = small[5:10, :] + acc_o[11:16, :]

    units = 8
    for u in range(units):
        s_send[u] = small[8 * (u // 4) : 8 * (u // 4) + 8, 128 * (u % 4) : 128 * (u % 4) + 128]
    lane_of = me * 2 + core
    unit = me // 2
    holder = (lax.rem(me, 2) == 0) & (core == lax.rem(unit, 2))

    @pl.loop(0, units)
    def _(u):
        to_core = lax.rem(u, 2)

        @pl.when((me == 2 * u) & (core == to_core))
        def _():
            s_recv[lane_of] = s_send[u]

        @pl.when((me != 2 * u) | (core != to_core))
        def _():
            send(s_send.at[u], s_recv.at[lane_of], s1_ss.at[u], s1_rs.at[lane_of],
                 (2 * u, 2 * z + to_core)).start()

    xa[...] = x_rows(half_sum.at[0], px)
    ya[...] = y_lanes(half_sum.at[1], py)
    for k in range(1, SIDE):
        x_copy(k).wait()
        xa[...] += x_recv[k].astype(F32)
    for k in range(1, SIDE):
        y2_send[k] = y_lanes(xa, peer_y(k)).astype(BF16)
        y2_copy(k).start()
    for k in range(1, SIDE):
        y_copy(k).wait()
        ya[...] += y_recv[k].astype(F32)
    for k in range(1, SIDE):
        x2_send[k] = x_rows(ya, peer_x(k)).astype(BF16)
        x2_copy(k).start()

    def u_copy(k, slot_at):
        return send(u_val, u_recv.at[slot_at], s2_ss.at[k], s2_rs.at[slot_at], (me, 2 * k + core))

    @pl.when(holder)
    def _():
        @pl.loop(0, 2 * planes)
        def _(i):
            @pl.when(i != lane_of)
            def _():
                send(s_send.at[0], s_recv.at[i], s1_ss.at[0], s1_rs.at[i],
                     (i // 2, 2 * z + lax.rem(i, 2))).wait_recv()

        u_val[...] = jnp.sum(s_recv[...], axis=0)

        @pl.loop(0, depth)
        def _(k):
            @pl.when(k != z)
            def _():
                u_copy(k, z).start()

    part[0:hz] = y_lanes(xa, py).reshape(hz, rx, 128)
    for k in range(1, SIDE):
        y2_copy(k).wait()
        part[0:hz] += y2_recv[k].astype(F32).reshape(hz, rx, 128)
    part[hz:] = x_rows(ya, px).reshape(hz, rx, 128)
    for k in range(1, SIDE):
        x2_copy(k).wait()
        part[hz:] += x2_recv[k].astype(F32).reshape(hz, rx, 128)
    pad = z_send.shape[1] - rx
    padding = [jnp.zeros((zhalf, pad, 128), F32)] if pad else []
    z_send[...] = jnp.concatenate([part[...]] + padding, axis=1).astype(BF16)

    def z_copy(i, slot_at):
        return send(z_send.at[i], z_recv.at[slot_at], z_ss.at[i], z_rs.at[slot_at],
                    (me, 2 * (core * zhalf + i) + core))

    @pl.loop(0, zhalf)
    def _(i):
        @pl.when(core * zhalf + i != z)
        def _():
            z_copy(i, z).start()

    def v_copy(i, slot_at):
        return send(v_val, v_recv.at[slot_at], s3_ss.at[i], s3_rs.at[slot_at],
                    (i // 2, 2 * z + lax.rem(i, 2)))

    @pl.when(holder)
    def _():
        v_val[...] = u_val[...]

        @pl.loop(0, depth)
        def _(k):
            @pl.when(k != z)
            def _():
                u_copy(k, k).wait_recv()
                v_val[...] += u_recv[k]

        v_recv[unit] = v_val[...]

        @pl.loop(0, 2 * planes)
        def _(i):
            @pl.when(i != lane_of)
            def _():
                v_copy(i, unit).start()

    active = z // zhalf == core
    to_core = px // 2
    mine_at = lax.rem(px, 2) * SIDE + py

    def d_copy(p, slot_at):
        return send(full, gathered.at[slot_at], d_ss.at[p], d_rs.at[slot_at], (p, 2 * z + to_core))

    @pl.when(active)
    def _():
        full[...] = part[lax.rem(z, zhalf)]

        @pl.loop(0, depth)
        def _(k):
            @pl.when(k != z)
            def _():
                send(z_send.at[0], z_recv.at[k], z_ss.at[0], z_rs.at[k],
                     (me, 2 * k + core)).wait_recv()
                full[...] += z_recv[k].astype(F32)[0:rx]

        @pl.when(to_core == core)
        def _():
            gathered[mine_at] = full[...]

        @pl.loop(0, planes)
        def _(p):
            @pl.when((p != me) | (to_core != core))
            def _():
                d_copy(p, mine_at).start()

    for u in range(units):
        @pl.when((me != 2 * u) | (core != u % 2))
        def _(u=u):
            v_copy(0, u).wait_recv()
    for u in range(units):
        cols = slice(128 * (u % 4), 128 * (u % 4) + 128)
        if u < 4:
            first_out[0:8, cols] = v_recv[u]
        else:
            first_out[8:10, cols] = v_recv[u, 0:2]
            norm_out[:, cols] = v_recv[u, 2:4]

    owner = z // zhalf
    for i in range(2):
        for y in range(SIDE):
            sender = y * SIDE + 2 * core + i

            @pl.when((sender != me) | (owner != core))
            def _(i=i, y=y):
                send(full, gathered.at[i * SIDE + y], d_ss.at[0], d_rs.at[i * SIDE + y],
                     (me, dy + 1 - 2 * core)).wait_recv()
            second_out[rx * i : rx * i + rx, 128 * y : 128 * y + 128] = gathered[i * SIDE + y]

    @pl.loop(0, units)
    def _(u):
        @pl.when((me != 2 * u) | (core != lax.rem(u, 2)))
        def _():
            send(s_send.at[u], s_recv.at[lane_of], s1_ss.at[u], s1_rs.at[lane_of],
                 (2 * u, 2 * z + lax.rem(u, 2))).wait_send()

    @pl.when(holder)
    def _():
        @pl.loop(0, depth)
        def _(k):
            @pl.when(k != z)
            def _():
                u_copy(k, z).wait_send()

        @pl.loop(0, 2 * planes)
        def _(i):
            @pl.when(i != lane_of)
            def _():
                v_copy(i, unit).wait_send()

    @pl.loop(0, zhalf)
    def _(i):
        @pl.when(core * zhalf + i != z)
        def _():
            z_copy(i, z).wait_send()

    @pl.when(active)
    def _():
        @pl.loop(0, planes)
        def _(p):
            @pl.when((p != me) | (to_core != core))
            def _():
                d_copy(p, mine_at).wait_send()


def on_device(audio, counts, cotangent, conv_first, norm_gain, norm_bias, conv_second):
    planes = lax.axis_size("dx")
    groups = lax.axis_size("dy")
    depth = groups // 2
    crops, frames, channels = cotangent.shape[1:]
    rows_all = conv_second.shape[0]
    scale = 1.0 / math.sqrt(planes * groups * crops * frames)
    zhalf = depth // 2
    hz = zhalf // 2
    half_rows = rows_all // 2
    hrows = half_rows // 2
    rx = rows_all // depth // SIDE
    rpad = -(-rx // 16) * 16
    vm = pltpu.VMEM
    dma = pltpu.SemaphoreType.DMA
    scratch = [
        vm(audio.shape, BF16), vm(cotangent.shape, BF16), vm(conv_first.shape, BF16),
        vm((channels,), F32), vm((channels,), F32), vm(conv_second.shape, BF16), dma((6,)),
        vm((640, 640), BF16), vm((8, 16, 256), F32), vm((planes, 1, 128), jnp.int32),
        vm((planes, 16, 256), BF16), vm((planes, 16, 256), BF16),
        vm((16 * crops, 256), F32), vm((16 * crops, 256), BF16),
        vm((16, 2 * channels), F32), vm((128, channels), F32),
        vm((crops, 192, 2 * channels), BF16), vm((crops, 16, 2 * channels), F32),
        vm((crops, 8, channels), F32), vm((crops, 16, 128), F32),
        vm((2, crops * frames, half_rows), BF16), vm((crops * frames, channels), BF16),
        vm((crops, frames, channels), F32), vm((crops, frames, channels), F32),
        vm((crops, 1, channels), F32), vm((frames + 8, channels), F32),
        vm((frames + 8, channels), F32),
        vm((2, hrows, channels), F32), vm((2, hrows, channels), BF16),
        vm((2, hrows, channels), BF16),
        vm((SIDE, hz * rx, channels), BF16), vm((SIDE, hz * rx, channels), BF16),
        vm((SIDE, hrows, 128), BF16), vm((SIDE, hrows, 128), BF16),
        vm((hz * rx, channels), F32), vm((hrows, 128), F32),
        vm((SIDE, hz * rx, 128), BF16), vm((SIDE, hz * rx, 128), BF16),
        vm((SIDE, hz * rx, 128), BF16), vm((SIDE, hz * rx, 128), BF16),
        vm((zhalf, rx, 128), F32), vm((zhalf, rpad, 128), BF16), vm((depth, rpad, 128), BF16),
        vm((rx, 128), F32), vm((8, rx, 128), F32),
        vm((16, channels), F32), vm((16, channels), F32), vm((8, channels), F32),
        vm((16, channels), F32), vm((8, 8, 128), F32), vm((2 * planes, 8, 128), F32),
        vm((8, 128), F32), vm((depth, 8, 128), F32), vm((8, 128), F32), vm((8, 8, 128), F32),
        dma((planes,)), dma((planes,)), dma((planes,)), dma((planes,)), dma((2,)), dma((2,)),
        dma((16,)), dma((16,)), dma((zhalf,)), dma((depth,)), dma((planes,)), dma((8,)),
        dma((8,)), dma((2 * planes,)), dma((depth,)), dma((depth,)), dma((2 * planes,)), dma((8,)),
    ]
    hbm = pl.BlockSpec(memory_space=pl.ANY)
    vmem = pl.BlockSpec(memory_space=pltpu.VMEM)
    return tuple(pl.pallas_call(
        functools.partial(kernel, planes, depth, scale),
        out_shape=[
            jax.ShapeDtypeStruct(conv_first.shape, F32),
            jax.ShapeDtypeStruct((2, channels), F32),
            jax.ShapeDtypeStruct((rows_all // groups, channels), F32),
        ],
        in_specs=[hbm, pl.BlockSpec(memory_space=pltpu.SMEM), hbm, hbm, hbm, hbm, hbm],
        out_specs=[vmem] * 3,
        scratch_shapes=scratch,
        compiler_params=pltpu.CompilerParams(
            collective_id=0, has_side_effects=True, vmem_limit_bytes=50 * 2**20),
    )(audio, counts, cotangent, conv_first, norm_gain, norm_bias, conv_second))


def solution(mesh):
    in_specs = (P("dy", "dx", None), P("dy", "dx"), P("dy", "dx", None, None), P(), P(), P(), P())
    out_specs = (P(), P(), P("dy", None))
    return jax.shard_map(
        on_device, mesh=mesh, in_specs=in_specs, out_specs=out_specs, check_vma=False
    )
```

```python
import functools
import math

import jax
import jax.numpy as jnp
from jax import lax
from jax.experimental import pallas as pl
from jax.experimental.pallas import tpu as pltpu
from jax.sharding import PartitionSpec as P

F32 = jnp.float32
BF16 = jnp.bfloat16
MESH = pl.DeviceIdType.MESH
SIDE = 4
TN = (((0,), (0,)), ((), ()))
NT = (((1,), (1,)), ((), ()))
NN = (((1,), (0,)), ((), ()))
LOG2E = 1.4426950408889634


def dot(a, b, dims=NN):
    return lax.dot_general(a, b, dims, preferred_element_type=F32)


def pieces(value):
    high = value.astype(BF16)
    rest = value - high.astype(F32)
    mid = rest.astype(BF16)
    low = (rest - mid.astype(F32)).astype(BF16)
    return high, mid, low


def gelu_parts(value):
    cdf = 0.5 * lax.erf(value * 0.7071067811865476) + 0.5
    slope = cdf + value * (jnp.exp2(value * value * (-0.5 * LOG2E)) * 0.3989422804014327)
    return cdf, slope


def rows_of(shape):
    return lax.broadcasted_iota(jnp.int32, shape, 0)


def cols_of(shape):
    return lax.broadcasted_iota(jnp.int32, shape, 1)


def kernel(
    planes, depth, scale,
    audio_hbm, counts_hbm, cot_hbm, w1_hbm, gain_hbm, bias_hbm, w2_hbm,
    first_out, norm_out, second_out,
    audio, counts_ref, cot, w1, gain_ref, bias_ref, w2, load_sem,
    perm, zbuf, cnt_all, crop_send, crop_recv, xf, xp, weo, wpad, waug, gw, stat, colsum,
    hid, grows, slope_e, slope_o, slope_t, hshift, dshift,
    half_sum, pair_send, pair_recv, p_send, p_recv, part, z_send, z_recv, full, gathered,
    acc_e, acc_o, acc_t, small, s_send, s_recv, u_val, u_recv, v_val, v_recv,
    cnt_ss, cnt_rs, crop_ss, crop_rs, pair_ss, pair_rs, plane_ss, plane_rs,
    z_ss, z_rs, d_ss, d_rs, s1_ss, s1_rs, s2_ss, s2_rs, s3_ss, s3_rs,
):
    me = lax.axis_index("dx")
    dy = lax.axis_index("dy")
    core = lax.rem(dy, 2)
    z = dy // 2
    px = lax.rem(me, SIDE)
    py = me // SIDE
    zhalf = depth // 2
    frames = cot_hbm.shape[2]
    channels = w2_hbm.shape[1]
    rows_all = w2_hbm.shape[0]
    half_rows = rows_all // 2
    rz = rows_all // depth
    rx = rz // SIDE
    hz = zhalf // 2
    hrows = half_rows // 2
    total_frames = 2 * frames + 1
    crops = cot_hbm.shape[1]

    def send(src, dst, ss, rs, where):
        return pltpu.make_async_remote_copy(
            src_ref=src, dst_ref=dst, send_sem=ss, recv_sem=rs,
            device_id=where, device_id_type=MESH,
        )

    loads = [
        pltpu.make_async_copy(src, dst, load_sem.at[i])
        for i, (src, dst) in enumerate(
            ((audio_hbm, audio), (w1_hbm, w1), (gain_hbm, gain_ref), (bias_hbm, bias_ref),
             (w2_hbm, w2), (cot_hbm, cot), (counts_hbm, counts_ref))
        )
    ]
    for load in loads:
        load.start()

    barrier = pltpu.get_barrier_semaphore()

    @pl.loop(0, planes)
    def _(p):
        @pl.when(p != me)
        def _():
            pl.semaphore_signal(barrier, inc=1, device_id=(p, dy), device_id_type=MESH)

        pl.semaphore_signal(barrier, inc=1, device_id=(p, 2 * z + 1 - core), device_id_type=MESH)

    @pl.loop(0, depth)
    def _(k):
        @pl.when(k != z)
        def _():
            pl.semaphore_signal(barrier, inc=1, device_id=(me, 2 * k + core), device_id_type=MESH)

    lane = cols_of((1, 640))
    sample = 10 * (lane % 64) + 2 * (lane // 128) + (lane % 128) // 64
    for i in range(5):
        block = rows_of((128, 640)) + 128 * i
        perm[pl.ds(128 * i, 128), :] = jnp.where(block == sample, 1.0, 0.0).astype(BF16)
    loads[6].wait()
    cnt_all[me] = jnp.full((1, 128), counts_ref[0, 0], jnp.int32)

    loads[0].wait()
    blocks = jnp.concatenate(
        [audio[0, :, 640 * i : 640 * i + 640].astype(F32) for i in range(4)], axis=0
    ).astype(BF16)
    sorted_blocks = dot(blocks, perm[...])
    eye = jnp.where(rows_of((10, 256)) == cols_of((10, 256)), 1.0, 0.0).astype(BF16)
    tails = dot(audio[0, :, 2560:2570], eye)
    low_lane = cols_of((8, 128)) < 64
    last_lane = cols_of((8, 256)) == 255
    for m in range(10):
        g = m // 2
        parts = []
        for half in range(2):
            a = sorted_blocks[16 * half : 16 * half + 8, 128 * g : 128 * g + 128]
            b = sorted_blocks[16 * half + 8 : 16 * half + 16, 128 * g : 128 * g + 128]
            if m % 2 == 0:
                parts.append(jnp.where(low_lane, a, pltpu.roll(b, 64, 1)))
            else:
                parts.append(jnp.where(low_lane, pltpu.roll(a, 64, 1), b))
        row = jnp.concatenate(parts, axis=1)
        zbuf[:, m, :] = row
        if m < 5:
            zbuf[:, 11 + m, :] = jnp.where(last_lane, tails[:, m : m + 1], pltpu.roll(row, 255, 1))
    zbuf[:, 10, :] = tails
    slot_rows = zbuf[...].reshape(128, 256).astype(BF16)

    waug[...] = jnp.zeros_like(waug)
    loads[1].wait()
    loads[2].wait()
    loads[3].wait()
    w1v = w1[...].astype(F32)
    weo[...] = jnp.zeros_like(weo)
    weo[0:10, 0:channels] = w1v
    weo[5:10, channels:] = w1v[0:5]
    weo[11:16, channels:] = w1v[5:10]
    wpad[...] = jnp.zeros_like(wpad)
    wpad[0:10, :] = w1v

    pl.semaphore_wait(barrier, 2 * planes - 1 + depth - 1)

    @pl.loop(1, planes)
    def _(k):
        to = lax.rem(me + k, planes)
        send(cnt_all.at[me], cnt_all.at[me], cnt_ss.at[k], cnt_rs.at[k], (to, dy)).start()

    @pl.loop(1, planes)
    def _(k):
        frm = lax.rem(me - k + planes, planes)
        send(cnt_all.at[me], cnt_all.at[frm], cnt_ss.at[k], cnt_rs.at[k], (frm, dy)).wait()

    count_rows = cnt_all[...].reshape(planes, 128)
    who = rows_of((planes, 128))
    start_me = jnp.sum(jnp.where(who < me, count_rows, 0), axis=0, keepdims=True)
    count_me = jnp.sum(jnp.where(who == me, count_rows, 0), axis=0, keepdims=True)
    shape = (16 * planes, 128)
    rr, cc = rows_of(shape), cols_of(shape)
    slot = cc // 16
    pick = (rr % 16 == cc % 16) & (slot < count_me) & ((start_me + slot) % planes == rr // 16)
    routed = dot(jnp.where(pick, 1.0, 0.0).astype(BF16), slot_rows).astype(BF16)
    crop_send[...] = routed.reshape(planes, 16, 256)

    @pl.loop(1, planes)
    def _(k):
        to = lax.rem(me + k, planes)
        send(crop_send.at[to], crop_recv.at[me], crop_ss.at[k], crop_rs.at[k], (to, dy)).start()

    crop_recv[me] = crop_send[me]
    wide = jnp.concatenate([count_rows, count_rows], axis=1)
    who2, col2 = rows_of((planes, 256)), cols_of((planes, 256)) // 16
    start_col = jnp.sum(jnp.where(who2 < col2, wide, 0), axis=0, keepdims=True)
    count_col = jnp.sum(jnp.where(who2 == col2, wide, 0), axis=0, keepdims=True)
    shape = (16 * crops, 256)
    rr, cc = rows_of(shape), cols_of(shape)
    order = (rr // 16) * planes + me
    pick = (rr % 16 == cc % 16) & (start_col <= order) & (order < start_col + count_col)
    pick = jnp.where(pick, 1.0, 0.0).astype(BF16)

    @pl.loop(1, planes)
    def _(k):
        frm = lax.rem(me - k + planes, planes)
        send(crop_send.at[frm], crop_recv.at[frm], crop_ss.at[k], crop_rs.at[k], (frm, dy)).wait()

    mine = dot(pick, crop_recv[...].reshape(16 * planes, 256))
    xf[...] = mine
    xp_all = jnp.where(rows_of((16 * crops, 256)) % 16 == 10, 1.0, mine)
    xp[...] = xp_all.astype(BF16)
    xt = jnp.concatenate([xp_all] * 3, axis=0).T.astype(BF16)

    tail_rows = jnp.concatenate(
        [xf[16 * r + 10 : 16 * r + 11, 0:128] for r in range(crops)]
        + [jnp.zeros((8 - crops, 128), F32)], axis=0)
    tail_pre = dot(tail_rows.astype(BF16), wpad[...].astype(BF16))
    gain = gain_ref[...].reshape(1, channels)
    bias = bias_ref[...].reshape(1, channels)
    we, wo = weo[:, 0:channels], weo[:, channels:]
    weo16 = weo[...].astype(BF16)
    row16 = rows_of((16, channels))
    for r in range(crops):
        x16 = xp[16 * r : 16 * r + 16, :]
        gram = dot(x16, x16, NT)
        g1, g2, g3 = pieces(gram)
        gwv = dot(g1, weo16) + dot(g2, weo16) + dot(g3, weo16)
        gw[r] = gwv
        colsum[r] = jnp.broadcast_to(gram[:, 10:11], (16, 128))
        pre_t = tail_pre[r : r + 1]
        gwe, gwo = gwv[:, 0:channels], gwv[:, channels:]
        mu = (gwe[10:11] + gwo[10:11] + pre_t) * (1.0 / total_frames)
        square = jnp.sum(we * gwe + wo * gwo, axis=0, keepdims=True) + pre_t * pre_t
        var = jnp.maximum(square * (1.0 / total_frames) - mu * mu, 0.0)
        inv = lax.rsqrt(var + 1e-5)
        mul = inv * gain
        add = bias - mu * mul
        stat[r, 0:1] = mu
        stat[r, 1:2] = inv
        stat[r, 2:3] = mul
        stat[r, 3:4] = pre_t
        stat[r, 4:5] = pre_t * mul + add
        for side, w in ((0, we), (1, wo)):
            scaled = jnp.where(row16 == 10, add, w * mul)
            for i, piece in enumerate(pieces(scaled)):
                waug[r, 64 * i + 16 * r : 64 * i + 16 * r + 16,
                     side * channels : (side + 1) * channels] = piece

    loads[4].wait()
    loads[5].wait()
    quarter = channels // 2
    xt_parts = [xt[128 * i : 128 * i + 128] for i in range(frames // 128)]

    @pl.loop(0, crops)
    def _(r):
        base = pl.multiple_of(r * frames, frames)
        tail = stat[r, 4:5]
        cdf, slope = gelu_parts(tail)
        hshift[frames : frames + 1, :] = tail * cdf
        slope_t[r] = slope
        for n in range(4):
            for i in range(frames // 128):
                value = dot(xt_parts[i], waug[r, :, n * quarter : (n + 1) * quarter])
                cdf, slope = gelu_parts(value)
                value = value * cdf
                lo = (n % 2) * quarter
                if n < 2:
                    slope_e[r, 128 * i : 128 * i + 128, lo : lo + quarter] = slope
                    hshift[128 * i : 128 * i + 128, lo : lo + quarter] = value
                    hid[0, pl.ds(base + 128 * i, 128), lo : lo + quarter] = value.astype(BF16)
                else:
                    slope_o[r, 128 * i : 128 * i + 128, lo : lo + quarter] = slope
                    at = 512 if n == 2 else 0
                    hid[n - 2, pl.ds(base + 128 * i, 128), at : at + quarter] = value.astype(BF16)
        hid[1, pl.ds(base, frames), quarter:] = hshift[1 : frames + 1, :].astype(BF16)
        for n in range(2):
            cols = slice(n * quarter, (n + 1) * quarter)
            pre = dot(hid[0, pl.ds(base, frames), :], w2[0:half_rows, cols])
            pre = pre + dot(hid[1, pl.ds(base, frames), :], w2[half_rows:, cols])
            slope = gelu_parts(pre)[1]
            grad = (scale * cot[0, r, :, cols].astype(F32)) * slope
            grows[pl.ds(base, frames), cols] = grad.astype(BF16)

    pair = (me, 2 * z + 1 - core)
    for h in range(2):
        theirs = dot(hid[1 - core, :, h * hrows : (h + 1) * hrows], grows[...], TN)
        pair_send[h] = theirs.astype(BF16)
        send(pair_send.at[h], pair_recv.at[h], pair_ss.at[h], pair_rs.at[h], pair).start()
    for h in range(2):
        half_sum[h] = dot(hid[core, :, h * hrows : (h + 1) * hrows], grows[...], TN)

    def p_copy(h, k, slot, slot_at, where):
        return send(p_send.at[h, slot], p_recv.at[h, slot_at], plane_ss.at[h, k], plane_rs.at[h, k],
                    (where, dy))

    for h in range(2):
        send(pair_send.at[h], pair_recv.at[h], pair_ss.at[h], pair_rs.at[h], pair).wait()
        half_sum[h] = half_sum[h] + pair_recv[h].astype(F32)
        for p in range(planes):
            lanes = slice(128 * (p // SIDE), 128 * (p // SIDE) + 128)
            first = (p % SIDE) * rx
            p_send[h, p] = jnp.concatenate(
                [half_sum[h, i * rz + first : i * rz + first + rx, lanes] for i in range(hz)], axis=0
            ).astype(BF16)

        @pl.loop(1, planes)
        def _(k):
            to = lax.rem(me + k, planes)
            p_copy(h, k, to, me, to).start()

    acc_e[...] = jnp.zeros_like(acc_e)
    acc_o[...] = jnp.zeros_like(acc_o)
    acc_t[...] = jnp.zeros_like(acc_t)
    small[...] = jnp.zeros_like(small)
    dshift[0:8, :] = jnp.zeros((8, channels), F32)

    def backward(r):
        base = pl.multiple_of(r * frames, frames)
        grad = grows[pl.ds(base, frames), :]
        x16 = xp[pl.ds(pl.multiple_of(16 * r, 16), 16), :]
        shift_o = dot(grad, w2[channels : 2 * channels, :], NT) * slope_o[r]
        p_o = dot(x16, shift_o.astype(BF16))
        dshift[8 : 8 + frames, :] = dot(grad, w2[2 * channels :, :], NT)
        shift_e = dot(grad, w2[0:channels, :], NT) + dshift[7 : 7 + frames, :]
        p_e = dot(x16, (shift_e * slope_e[r]).astype(BF16))
        shift_t = dshift[7 + frames : 8 + frames, :] * slope_t[r]
        mu, inv, mul, pre_t = stat[r, 0:1], stat[r, 1:2], stat[r, 2:3], stat[r, 3:4]
        total = p_e[10:11] + p_o[10:11] + shift_t
        with_pre = jnp.sum(weo[:, 0:channels] * p_e + weo[:, channels:] * p_o, axis=0, keepdims=True)
        with_norm = inv * (with_pre + pre_t * shift_t - mu * total)
        small[10:11, :] = small[10:11, :] + with_norm
        small[11:12, :] = small[11:12, :] + total
        mean_g = total * (1.0 / total_frames)
        mean_n = with_norm * (1.0 / total_frames) * inv
        sums = jnp.concatenate([colsum[r]] * (channels // 128), axis=1)
        base_part = mean_g * sums
        acc_e[...] += mul * (p_e - base_part - mean_n * (gw[r, :, 0:channels] - mu * sums))
        acc_o[...] += mul * (p_o - base_part - mean_n * (gw[r, :, channels:] - mu * sums))
        acc_t[pl.ds(r, 1), :] = mul * (shift_t - mean_g - mean_n * (pre_t - mu))

    @pl.loop(0, crops)
    def _(r):
        backward(r)

    tail_grad = lax.dot_general(
        tail_rows, acc_t[...], TN, preferred_element_type=F32, precision=lax.Precision.HIGHEST)
    small[0:10, :] = acc_e[0:10, :] + tail_grad[0:10, :]
    small[0:5, :] = small[0:5, :] + acc_o[5:10, :]
    small[5:10, :] = small[5:10, :] + acc_o[11:16, :]

    units = 8
    for u in range(units):
        s_send[u] = small[8 * (u // 4) : 8 * (u // 4) + 8, 128 * (u % 4) : 128 * (u % 4) + 128]
    lane_of = me * 2 + core
    unit = me // 2
    holder = (lax.rem(me, 2) == 0) & (core == lax.rem(unit, 2))

    @pl.loop(0, units)
    def _(u):
        to_core = lax.rem(u, 2)

        @pl.when((me == 2 * u) & (core == to_core))
        def _():
            s_recv[lane_of] = s_send[u]

        @pl.when((me != 2 * u) | (core != to_core))
        def _():
            send(s_send.at[u], s_recv.at[lane_of], s1_ss.at[u], s1_rs.at[lane_of],
                 (2 * u, 2 * z + to_core)).start()

    mine_rows = pl.multiple_of(px * rx, 8)
    mine_lanes = pl.ds(pl.multiple_of(128 * py, 128), 128)
    pad = z_send.shape[1] - rx

    def z_copy(i, slot_at):
        return send(z_send.at[i], z_recv.at[slot_at], z_ss.at[i], z_rs.at[slot_at],
                    (me, 2 * (core * zhalf + i) + core))

    for h in range(2):
        own = jnp.concatenate(
            [half_sum[h, pl.ds(i * rz + mine_rows, rx), mine_lanes] for i in range(hz)], axis=0)

        def add(k, total):
            frm = lax.rem(me - k + planes, planes)
            p_copy(h, k, frm, frm, frm).wait()
            return total + p_recv[h, frm].astype(F32)

        own = lax.fori_loop(1, planes, add, own).reshape(hz, rx, 128)
        part[h * hz : h * hz + hz] = own
        padding = [jnp.zeros((hz, pad, 128), F32)] if pad else []
        z_send[h * hz : h * hz + hz] = jnp.concatenate([own] + padding, axis=1).astype(BF16)

        @pl.loop(h * hz, h * hz + hz)
        def _(i):
            @pl.when(core * zhalf + i != z)
            def _():
                z_copy(i, z).start()

    def u_copy(k, slot_at):
        return send(u_val, u_recv.at[slot_at], s2_ss.at[k], s2_rs.at[slot_at], (me, 2 * k + core))

    @pl.when(holder)
    def _():
        @pl.loop(0, 2 * planes)
        def _(i):
            @pl.when(i != lane_of)
            def _():
                send(s_send.at[0], s_recv.at[i], s1_ss.at[0], s1_rs.at[i],
                     (i // 2, 2 * z + lax.rem(i, 2))).wait_recv()

        u_val[...] = jnp.sum(s_recv[...], axis=0)

        @pl.loop(0, depth)
        def _(k):
            @pl.when(k != z)
            def _():
                u_copy(k, z).start()

    def v_copy(i, slot_at):
        return send(v_val, v_recv.at[slot_at], s3_ss.at[i], s3_rs.at[slot_at],
                    (i // 2, 2 * z + lax.rem(i, 2)))

    @pl.when(holder)
    def _():
        v_val[...] = u_val[...]

        @pl.loop(0, depth)
        def _(k):
            @pl.when(k != z)
            def _():
                u_copy(k, k).wait_recv()
                v_val[...] += u_recv[k]

        v_recv[unit] = v_val[...]

        @pl.loop(0, 2 * planes)
        def _(i):
            @pl.when(i != lane_of)
            def _():
                v_copy(i, unit).start()

    active = z // zhalf == core
    to_core = px // 2
    mine_at = lax.rem(px, 2) * SIDE + py

    def d_copy(p, slot_at):
        return send(full, gathered.at[slot_at], d_ss.at[p], d_rs.at[slot_at], (p, 2 * z + to_core))

    @pl.when(active)
    def _():
        full[...] = part[lax.rem(z, zhalf)]

        @pl.loop(0, depth)
        def _(k):
            @pl.when(k != z)
            def _():
                send(z_send.at[0], z_recv.at[k], z_ss.at[0], z_rs.at[k],
                     (me, 2 * k + core)).wait_recv()
                full[...] += z_recv[k].astype(F32)[0:rx]

        @pl.when(to_core == core)
        def _():
            gathered[mine_at] = full[...]

        @pl.loop(0, planes)
        def _(p):
            @pl.when((p != me) | (to_core != core))
            def _():
                d_copy(p, mine_at).start()

    for u in range(units):
        @pl.when((me != 2 * u) | (core != u % 2))
        def _(u=u):
            v_copy(0, u).wait_recv()
    for u in range(units):
        cols = slice(128 * (u % 4), 128 * (u % 4) + 128)
        if u < 4:
            first_out[0:8, cols] = v_recv[u]
        else:
            first_out[8:10, cols] = v_recv[u, 0:2]
            norm_out[:, cols] = v_recv[u, 2:4]

    owner = z // zhalf
    for i in range(2):
        for y in range(SIDE):
            sender = y * SIDE + 2 * core + i

            @pl.when((sender != me) | (owner != core))
            def _(i=i, y=y):
                send(full, gathered.at[i * SIDE + y], d_ss.at[0], d_rs.at[i * SIDE + y],
                     (me, dy + 1 - 2 * core)).wait_recv()
            second_out[rx * i : rx * i + rx, 128 * y : 128 * y + 128] = gathered[i * SIDE + y]

    @pl.loop(0, units)
    def _(u):
        @pl.when((me != 2 * u) | (core != lax.rem(u, 2)))
        def _():
            send(s_send.at[u], s_recv.at[lane_of], s1_ss.at[u], s1_rs.at[lane_of],
                 (2 * u, 2 * z + lax.rem(u, 2))).wait_send()

    @pl.when(holder)
    def _():
        @pl.loop(0, depth)
        def _(k):
            @pl.when(k != z)
            def _():
                u_copy(k, z).wait_send()

        @pl.loop(0, 2 * planes)
        def _(i):
            @pl.when(i != lane_of)
            def _():
                v_copy(i, unit).wait_send()

    @pl.loop(0, zhalf)
    def _(i):
        @pl.when(core * zhalf + i != z)
        def _():
            z_copy(i, z).wait_send()

    @pl.when(active)
    def _():
        @pl.loop(0, planes)
        def _(p):
            @pl.when((p != me) | (to_core != core))
            def _():
                d_copy(p, mine_at).wait_send()


def on_device(audio, counts, cotangent, conv_first, norm_gain, norm_bias, conv_second):
    planes = lax.axis_size("dx")
    groups = lax.axis_size("dy")
    depth = groups // 2
    crops, frames, channels = cotangent.shape[1:]
    rows_all = conv_second.shape[0]
    scale = 1.0 / math.sqrt(planes * groups * crops * frames)
    zhalf = depth // 2
    hz = zhalf // 2
    half_rows = rows_all // 2
    hrows = half_rows // 2
    rx = rows_all // depth // SIDE
    rpad = -(-rx // 16) * 16
    vm = pltpu.VMEM
    dma = pltpu.SemaphoreType.DMA
    scratch = [
        vm(audio.shape, BF16), pltpu.SMEM((1, 1), jnp.int32), vm(cotangent.shape, BF16), vm(conv_first.shape, BF16),
        vm((channels,), F32), vm((channels,), F32), vm(conv_second.shape, BF16), dma((7,)),
        vm((640, 640), BF16), vm((8, 16, 256), F32), vm((planes, 1, 128), jnp.int32),
        vm((planes, 16, 256), BF16), vm((planes, 16, 256), BF16),
        vm((16 * crops, 256), F32), vm((16 * crops, 256), BF16),
        vm((16, 2 * channels), F32), vm((128, channels), F32),
        vm((crops, 192, 2 * channels), BF16), vm((crops, 16, 2 * channels), F32),
        vm((crops, 8, channels), F32), vm((crops, 16, 128), F32),
        vm((2, crops * frames, half_rows), BF16), vm((crops * frames, channels), BF16),
        vm((crops, frames, channels), F32), vm((crops, frames, channels), F32),
        vm((crops, 1, channels), F32), vm((frames + 8, channels), F32),
        vm((frames + 8, channels), F32),
        vm((2, hrows, channels), F32), vm((2, hrows, channels), BF16),
        vm((2, hrows, channels), BF16),
        vm((2, planes, hz * rx, 128), BF16), vm((2, planes, hz * rx, 128), BF16),
        vm((zhalf, rx, 128), F32), vm((zhalf, rpad, 128), BF16), vm((depth, rpad, 128), BF16),
        vm((rx, 128), F32), vm((8, rx, 128), F32),
        vm((16, channels), F32), vm((16, channels), F32), vm((8, channels), F32),
        vm((16, channels), F32), vm((8, 8, 128), F32), vm((2 * planes, 8, 128), F32),
        vm((8, 128), F32), vm((depth, 8, 128), F32), vm((8, 128), F32), vm((8, 8, 128), F32),
        dma((planes,)), dma((planes,)), dma((planes,)), dma((planes,)), dma((2,)), dma((2,)),
        dma((2, planes)), dma((2, planes)), dma((zhalf,)), dma((depth,)), dma((planes,)), dma((8,)),
        dma((8,)), dma((2 * planes,)), dma((depth,)), dma((depth,)), dma((2 * planes,)), dma((8,)),
    ]
    hbm = pl.BlockSpec(memory_space=pltpu.HBM)
    vmem = pl.BlockSpec(memory_space=pltpu.VMEM)
    outs = pl.pallas_call(
        functools.partial(kernel, planes, depth, scale),
        out_shape=[
            jax.ShapeDtypeStruct(conv_first.shape, F32),
            jax.ShapeDtypeStruct((2, channels), F32),
            jax.ShapeDtypeStruct((rows_all // groups, channels), F32),
        ],
        in_specs=[hbm, hbm, hbm, hbm, hbm, hbm, hbm],
        out_specs=[vmem] * 3,
        scratch_shapes=scratch,
        compiler_params=pltpu.CompilerParams(
            collective_id=0, has_side_effects=True, vmem_limit_bytes=63 * 2**20),
    )(audio, counts, cotangent, conv_first, norm_gain, norm_bias, conv_second)

    def place(*refs):
        ins, results, held, sems = refs[0:3], refs[3:6], refs[6:9], refs[9]
        reads = [pltpu.make_async_copy(ins[i], held[i], sems.at[i]) for i in range(3)]
        writes = [pltpu.make_async_copy(held[i], results[i], sems.at[3 + i]) for i in range(3)]
        for read in reads:
            read.start()
        for read, write in zip(reads, writes):
            read.wait()
            write.start()
        for write in writes:
            write.wait()

    return tuple(pl.pallas_call(
        place,
        out_shape=[jax.ShapeDtypeStruct(out.shape, out.dtype) for out in outs],
        in_specs=[hbm] * 3,
        out_specs=[pl.BlockSpec(memory_space=pltpu.HBM)] * 3,
        scratch_shapes=[vm(out.shape, F32) for out in outs] + [dma((6,))],
        compiler_params=pltpu.CompilerParams(vmem_limit_bytes=63 * 2**20),
    )(*outs))


def solution(mesh):
    in_specs = (P("dy", "dx", None), P("dy", "dx"), P("dy", "dx", None, None), P(), P(), P(), P())
    out_specs = (P(), P(), P("dy", None))
    return jax.shard_map(
        on_device, mesh=mesh, in_specs=in_specs, out_specs=out_specs, check_vma=False
    )
```

```python
import functools
import math

import jax
import jax.numpy as jnp
from jax import lax
from jax.experimental import pallas as pl
from jax.experimental.pallas import tpu as pltpu
from jax.sharding import PartitionSpec as P

F32 = jnp.float32
BF16 = jnp.bfloat16
MESH = pl.DeviceIdType.MESH
SIDE = 4
TN = (((0,), (0,)), ((), ()))
NT = (((1,), (1,)), ((), ()))
NN = (((1,), (0,)), ((), ()))
LOG2E = 1.4426950408889634


def dot(a, b, dims=NN):
    return lax.dot_general(a, b, dims, preferred_element_type=F32)


def pieces(value):
    high = value.astype(BF16)
    rest = value - high.astype(F32)
    mid = rest.astype(BF16)
    low = (rest - mid.astype(F32)).astype(BF16)
    return high, mid, low


def gelu_parts(value):
    cdf = 0.5 * lax.erf(value * 0.7071067811865476) + 0.5
    slope = cdf + value * (jnp.exp2(value * value * (-0.5 * LOG2E)) * 0.3989422804014327)
    return cdf, slope


def rows_of(shape):
    return lax.broadcasted_iota(jnp.int32, shape, 0)


def cols_of(shape):
    return lax.broadcasted_iota(jnp.int32, shape, 1)


def kernel(
    planes, depth, scale,
    audio_hbm, counts_ref, cot_hbm, w1_hbm, gain_hbm, bias_hbm, w2_hbm,
    first_out, norm_out, second_out,
    audio, cot, w1, gain_ref, bias_ref, w2, load_sem,
    perm, zbuf, cnt_all, crop_send, crop_recv, xf, xp, weo, wpad, waug, gw, stat, colsum,
    hid, grows, slope_e, slope_o, slope_t, hshift, dshift,
    half_sum, pair_send, pair_recv, p_send, p_recv, part, z_send, z_recv, full, gathered,
    acc_e, acc_o, acc_t, small, s_send, s_recv, u_val, u_recv, v_val, v_recv,
    cnt_ss, cnt_rs, crop_ss, crop_rs, pair_ss, pair_rs, plane_ss, plane_rs,
    z_ss, z_rs, d_ss, d_rs, s1_ss, s1_rs, s2_ss, s2_rs, s3_ss, s3_rs,
):
    me = lax.axis_index("dx")
    dy = lax.axis_index("dy")
    core = lax.rem(dy, 2)
    z = dy // 2
    px = lax.rem(me, SIDE)
    py = me // SIDE
    zhalf = depth // 2
    frames = cot_hbm.shape[2]
    channels = w2_hbm.shape[1]
    rows_all = w2_hbm.shape[0]
    half_rows = rows_all // 2
    rz = rows_all // depth
    rx = rz // SIDE
    hz = zhalf // 2
    hrows = half_rows // 2
    total_frames = 2 * frames + 1
    crops = cot_hbm.shape[1]

    def send(src, dst, ss, rs, where):
        return pltpu.make_async_remote_copy(
            src_ref=src, dst_ref=dst, send_sem=ss, recv_sem=rs,
            device_id=where, device_id_type=MESH,
        )

    loads = [
        pltpu.make_async_copy(src, dst, load_sem.at[i])
        for i, (src, dst) in enumerate(
            ((audio_hbm, audio), (w1_hbm, w1), (gain_hbm, gain_ref), (bias_hbm, bias_ref),
             (w2_hbm, w2), (cot_hbm, cot))
        )
    ]
    for load in loads:
        load.start()

    barrier = pltpu.get_barrier_semaphore()

    @pl.loop(0, planes)
    def _(p):
        @pl.when(p != me)
        def _():
            pl.semaphore_signal(barrier, inc=1, device_id=(p, dy), device_id_type=MESH)

        pl.semaphore_signal(barrier, inc=1, device_id=(p, 2 * z + 1 - core), device_id_type=MESH)

    @pl.loop(0, depth)
    def _(k):
        @pl.when(k != z)
        def _():
            pl.semaphore_signal(barrier, inc=1, device_id=(me, 2 * k + core), device_id_type=MESH)

    lane = cols_of((1, 640))
    sample = 10 * (lane % 64) + 2 * (lane // 128) + (lane % 128) // 64
    for i in range(5):
        block = rows_of((128, 640)) + 128 * i
        perm[pl.ds(128 * i, 128), :] = jnp.where(block == sample, 1.0, 0.0).astype(BF16)
    cnt_all[me] = counts_ref[...]

    loads[0].wait()
    blocks = jnp.concatenate(
        [audio[0, :, 640 * i : 640 * i + 640].astype(F32) for i in range(4)], axis=0
    ).astype(BF16)
    sorted_blocks = dot(blocks, perm[...])
    eye = jnp.where(rows_of((10, 256)) == cols_of((10, 256)), 1.0, 0.0).astype(BF16)
    tails = dot(audio[0, :, 2560:2570], eye)
    low_lane = cols_of((8, 128)) < 64
    last_lane = cols_of((8, 256)) == 255
    for m in range(10):
        g = m // 2
        parts = []
        for half in range(2):
            a = sorted_blocks[16 * half : 16 * half + 8, 128 * g : 128 * g + 128]
            b = sorted_blocks[16 * half + 8 : 16 * half + 16, 128 * g : 128 * g + 128]
            if m % 2 == 0:
                parts.append(jnp.where(low_lane, a, pltpu.roll(b, 64, 1)))
            else:
                parts.append(jnp.where(low_lane, pltpu.roll(a, 64, 1), b))
        row = jnp.concatenate(parts, axis=1)
        zbuf[:, m, :] = row
        if m < 5:
            zbuf[:, 11 + m, :] = jnp.where(last_lane, tails[:, m : m + 1], pltpu.roll(row, 255, 1))
    zbuf[:, 10, :] = tails
    slot_rows = zbuf[...].reshape(128, 256).astype(BF16)

    waug[...] = jnp.zeros_like(waug)
    loads[1].wait()
    loads[2].wait()
    loads[3].wait()
    w1v = w1[...].astype(F32)
    weo[...] = jnp.zeros_like(weo)
    weo[0:10, 0:channels] = w1v
    weo[5:10, channels:] = w1v[0:5]
    weo[11:16, channels:] = w1v[5:10]
    wpad[...] = jnp.zeros_like(wpad)
    wpad[0:10, :] = w1v

    pl.semaphore_wait(barrier, 2 * planes - 1 + depth - 1)

    @pl.loop(1, planes)
    def _(k):
        to = lax.rem(me + k, planes)
        send(cnt_all.at[me], cnt_all.at[me], cnt_ss.at[k], cnt_rs.at[k], (to, dy)).start()

    @pl.loop(1, planes)
    def _(k):
        frm = lax.rem(me - k + planes, planes)
        send(cnt_all.at[me], cnt_all.at[frm], cnt_ss.at[k], cnt_rs.at[k], (frm, dy)).wait()

    count_rows = cnt_all[...].reshape(planes, 128)
    who = rows_of((planes, 128))
    start_me = jnp.sum(jnp.where(who < me, count_rows, 0), axis=0, keepdims=True)
    count_me = jnp.sum(jnp.where(who == me, count_rows, 0), axis=0, keepdims=True)
    shape = (16 * planes, 128)
    rr, cc = rows_of(shape), cols_of(shape)
    slot = cc // 16
    pick = (rr % 16 == cc % 16) & (slot < count_me) & ((start_me + slot) % planes == rr // 16)
    routed = dot(jnp.where(pick, 1.0, 0.0).astype(BF16), slot_rows).astype(BF16)
    crop_send[...] = routed.reshape(planes, 16, 256)

    @pl.loop(1, planes)
    def _(k):
        to = lax.rem(me + k, planes)
        send(crop_send.at[to], crop_recv.at[me], crop_ss.at[k], crop_rs.at[k], (to, dy)).start()

    crop_recv[me] = crop_send[me]
    wide = jnp.concatenate([count_rows, count_rows], axis=1)
    who2, col2 = rows_of((planes, 256)), cols_of((planes, 256)) // 16
    start_col = jnp.sum(jnp.where(who2 < col2, wide, 0), axis=0, keepdims=True)
    count_col = jnp.sum(jnp.where(who2 == col2, wide, 0), axis=0, keepdims=True)
    shape = (16 * crops, 256)
    rr, cc = rows_of(shape), cols_of(shape)
    order = (rr // 16) * planes + me
    pick = (rr % 16 == cc % 16) & (start_col <= order) & (order < start_col + count_col)
    pick = jnp.where(pick, 1.0, 0.0).astype(BF16)

    @pl.loop(1, planes)
    def _(k):
        frm = lax.rem(me - k + planes, planes)
        send(crop_send.at[frm], crop_recv.at[frm], crop_ss.at[k], crop_rs.at[k], (frm, dy)).wait()

    mine = dot(pick, crop_recv[...].reshape(16 * planes, 256))
    xf[...] = mine
    xp_all = jnp.where(rows_of((16 * crops, 256)) % 16 == 10, 1.0, mine)
    xp[...] = xp_all.astype(BF16)
    xt = jnp.concatenate([xp_all] * 3, axis=0).T.astype(BF16)

    tail_rows = jnp.concatenate(
        [xf[16 * r + 10 : 16 * r + 11, 0:128] for r in range(crops)]
        + [jnp.zeros((8 - crops, 128), F32)], axis=0)
    tail_pre = dot(tail_rows.astype(BF16), wpad[...].astype(BF16))
    gain = gain_ref[...].reshape(1, channels)
    bias = bias_ref[...].reshape(1, channels)
    we, wo = weo[:, 0:channels], weo[:, channels:]
    weo16 = weo[...].astype(BF16)
    row16 = rows_of((16, channels))
    for r in range(crops):
        x16 = xp[16 * r : 16 * r + 16, :]
        gram = dot(x16, x16, NT)
        g1, g2, g3 = pieces(gram)
        gwv = dot(g1, weo16) + dot(g2, weo16) + dot(g3, weo16)
        gw[r] = gwv
        colsum[r] = jnp.broadcast_to(gram[:, 10:11], (16, 128))
        pre_t = tail_pre[r : r + 1]
        gwe, gwo = gwv[:, 0:channels], gwv[:, channels:]
        mu = (gwe[10:11] + gwo[10:11] + pre_t) * (1.0 / total_frames)
        square = jnp.sum(we * gwe + wo * gwo, axis=0, keepdims=True) + pre_t * pre_t
        var = jnp.maximum(square * (1.0 / total_frames) - mu * mu, 0.0)
        inv = lax.rsqrt(var + 1e-5)
        mul = inv * gain
        add = bias - mu * mul
        stat[r, 0:1] = mu
        stat[r, 1:2] = inv
        stat[r, 2:3] = mul
        stat[r, 3:4] = pre_t
        stat[r, 4:5] = pre_t * mul + add
        for side, w in ((0, we), (1, wo)):
            scaled = jnp.where(row16 == 10, add, w * mul)
            for i, piece in enumerate(pieces(scaled)):
                waug[r, 64 * i + 16 * r : 64 * i + 16 * r + 16,
                     side * channels : (side + 1) * channels] = piece

    loads[4].wait()
    loads[5].wait()
    quarter = channels // 2
    xt_parts = [xt[128 * i : 128 * i + 128] for i in range(frames // 128)]

    for r in range(crops):
        base = pl.multiple_of(r * frames, frames)
        tail = stat[r, 4:5]
        cdf, slope = gelu_parts(tail)
        hshift[frames : frames + 1, :] = tail * cdf
        slope_t[r] = slope
        for n in range(4):
            for i in range(frames // 128):
                value = dot(xt_parts[i], waug[r, :, n * quarter : (n + 1) * quarter])
                cdf, slope = gelu_parts(value)
                value = value * cdf
                lo = (n % 2) * quarter
                if n < 2:
                    slope_e[r, 128 * i : 128 * i + 128, lo : lo + quarter] = slope
                    hshift[128 * i : 128 * i + 128, lo : lo + quarter] = value
                    hid[0, pl.ds(base + 128 * i, 128), lo : lo + quarter] = value.astype(BF16)
                else:
                    slope_o[r, 128 * i : 128 * i + 128, lo : lo + quarter] = slope
                    at = 512 if n == 2 else 0
                    hid[n - 2, pl.ds(base + 128 * i, 128), at : at + quarter] = value.astype(BF16)
        hid[1, pl.ds(base, frames), quarter:] = hshift[1 : frames + 1, :].astype(BF16)
        for n in range(2):
            cols = slice(n * quarter, (n + 1) * quarter)
            pre = dot(hid[0, pl.ds(base, frames), :], w2[0:half_rows, cols])
            pre = pre + dot(hid[1, pl.ds(base, frames), :], w2[half_rows:, cols])
            slope = gelu_parts(pre)[1]
            grad = (scale * cot[0, r, :, cols].astype(F32)) * slope
            grows[pl.ds(base, frames), cols] = grad.astype(BF16)

    pair = (me, 2 * z + 1 - core)
    for h in range(2):
        theirs = dot(hid[1 - core, :, h * hrows : (h + 1) * hrows], grows[...], TN)
        pair_send[h] = theirs.astype(BF16)
        send(pair_send.at[h], pair_recv.at[h], pair_ss.at[h], pair_rs.at[h], pair).start()
        if h == 0:
            half_sum[0] = dot(hid[core, :, 0:hrows], grows[...], TN)

    def p_copy(h, k, slot, slot_at, where):
        return send(p_send.at[h, slot], p_recv.at[h, slot_at], plane_ss.at[h, k], plane_rs.at[h, k],
                    (where, dy))

    for h in range(2):
        if h == 1:
            half_sum[1] = dot(hid[core, :, hrows:], grows[...], TN)
        send(pair_send.at[h], pair_recv.at[h], pair_ss.at[h], pair_rs.at[h], pair).wait()
        half_sum[h] = half_sum[h] + pair_recv[h].astype(F32)
        for p in range(planes):
            lanes = slice(128 * (p // SIDE), 128 * (p // SIDE) + 128)
            first = (p % SIDE) * rx
            p_send[h, p] = jnp.concatenate(
                [half_sum[h, i * rz + first : i * rz + first + rx, lanes] for i in range(hz)], axis=0
            ).astype(BF16)

        @pl.loop(1, planes)
        def _(k):
            to = lax.rem(me + k, planes)
            p_copy(h, k, to, me, to).start()

    acc_e[...] = jnp.zeros_like(acc_e)
    acc_o[...] = jnp.zeros_like(acc_o)
    acc_t[...] = jnp.zeros_like(acc_t)
    small[...] = jnp.zeros_like(small)
    dshift[0:8, :] = jnp.zeros((8, channels), F32)

    def backward(r):
        base = pl.multiple_of(r * frames, frames)
        grad = grows[pl.ds(base, frames), :]
        x16 = xp[pl.ds(pl.multiple_of(16 * r, 16), 16), :]
        shift_o = dot(grad, w2[channels : 2 * channels, :], NT) * slope_o[r]
        p_o = dot(x16, shift_o.astype(BF16))
        dshift[8 : 8 + frames, :] = dot(grad, w2[2 * channels :, :], NT)
        shift_e = dot(grad, w2[0:channels, :], NT) + dshift[7 : 7 + frames, :]
        p_e = dot(x16, (shift_e * slope_e[r]).astype(BF16))
        shift_t = dshift[7 + frames : 8 + frames, :] * slope_t[r]
        mu, inv, mul, pre_t = stat[r, 0:1], stat[r, 1:2], stat[r, 2:3], stat[r, 3:4]
        total = p_e[10:11] + p_o[10:11] + shift_t
        with_pre = jnp.sum(weo[:, 0:channels] * p_e + weo[:, channels:] * p_o, axis=0, keepdims=True)
        with_norm = inv * (with_pre + pre_t * shift_t - mu * total)
        small[10:11, :] = small[10:11, :] + with_norm
        small[11:12, :] = small[11:12, :] + total
        mean_g = total * (1.0 / total_frames)
        mean_n = with_norm * (1.0 / total_frames) * inv
        sums = jnp.concatenate([colsum[r]] * (channels // 128), axis=1)
        base_part = mean_g * sums
        acc_e[...] += mul * (p_e - base_part - mean_n * (gw[r, :, 0:channels] - mu * sums))
        acc_o[...] += mul * (p_o - base_part - mean_n * (gw[r, :, channels:] - mu * sums))
        acc_t[pl.ds(r, 1), :] = mul * (shift_t - mean_g - mean_n * (pre_t - mu))

    for r in range(crops):
        backward(r)

    tail_grad = lax.dot_general(
        tail_rows, acc_t[...], TN, preferred_element_type=F32, precision=lax.Precision.HIGHEST)
    small[0:10, :] = acc_e[0:10, :] + tail_grad[0:10, :]
    small[0:5, :] = small[0:5, :] + acc_o[5:10, :]
    small[5:10, :] = small[5:10, :] + acc_o[11:16, :]

    units = 8
    for u in range(units):
        s_send[u] = small[8 * (u // 4) : 8 * (u // 4) + 8, 128 * (u % 4) : 128 * (u % 4) + 128]
    lane_of = me * 2 + core
    unit = me // 2
    holder = (lax.rem(me, 2) == 0) & (core == lax.rem(unit, 2))

    @pl.loop(0, units)
    def _(u):
        to_core = lax.rem(u, 2)

        @pl.when((me == 2 * u) & (core == to_core))
        def _():
            s_recv[lane_of] = s_send[u]

        @pl.when((me != 2 * u) | (core != to_core))
        def _():
            send(s_send.at[u], s_recv.at[lane_of], s1_ss.at[u], s1_rs.at[lane_of],
                 (2 * u, 2 * z + to_core)).start()

    def u_copy(k, slot_at):
        return send(u_val, u_recv.at[slot_at], s2_ss.at[k], s2_rs.at[slot_at], (me, 2 * k + core))

    @pl.when(holder)
    def _():
        @pl.loop(0, 2 * planes)
        def _(i):
            @pl.when(i != lane_of)
            def _():
                send(s_send.at[0], s_recv.at[i], s1_ss.at[0], s1_rs.at[i],
                     (i // 2, 2 * z + lax.rem(i, 2))).wait_recv()

        u_val[...] = jnp.sum(s_recv[...], axis=0)

        @pl.loop(0, depth)
        def _(k):
            @pl.when(k != z)
            def _():
                u_copy(k, z).start()

    mine_rows = pl.multiple_of(px * rx, 8)
    mine_lanes = pl.ds(pl.multiple_of(128 * py, 128), 128)
    pad = z_send.shape[1] - rx

    def z_copy(i, slot_at):
        return send(z_send.at[i], z_recv.at[slot_at], z_ss.at[i], z_rs.at[slot_at],
                    (me, 2 * (core * zhalf + i) + core))

    for h in range(2):
        own = jnp.concatenate(
            [half_sum[h, pl.ds(i * rz + mine_rows, rx), mine_lanes] for i in range(hz)], axis=0)

        def add(k, total):
            frm = lax.rem(me - k + planes, planes)
            p_copy(h, k, frm, frm, frm).wait()
            return total + p_recv[h, frm].astype(F32)

        own = lax.fori_loop(1, planes, add, own).reshape(hz, rx, 128)
        part[h * hz : h * hz + hz] = own
        padding = [jnp.zeros((hz, pad, 128), F32)] if pad else []
        z_send[h * hz : h * hz + hz] = jnp.concatenate([own] + padding, axis=1).astype(BF16)

        @pl.loop(h * hz, h * hz + hz)
        def _(i):
            @pl.when(core * zhalf + i != z)
            def _():
                z_copy(i, z).start()

    def v_copy(i, slot_at):
        return send(v_val, v_recv.at[slot_at], s3_ss.at[i], s3_rs.at[slot_at],
                    (i // 2, 2 * z + lax.rem(i, 2)))

    @pl.when(holder)
    def _():
        v_val[...] = u_val[...]

        @pl.loop(0, depth)
        def _(k):
            @pl.when(k != z)
            def _():
                u_copy(k, k).wait_recv()
                v_val[...] += u_recv[k]

        v_recv[unit] = v_val[...]

        @pl.loop(0, 2 * planes)
        def _(i):
            @pl.when(i != lane_of)
            def _():
                v_copy(i, unit).start()

    active = z // zhalf == core
    to_core = px // 2
    mine_at = lax.rem(px, 2) * SIDE + py

    def d_copy(p, slot_at):
        return send(full, gathered.at[slot_at], d_ss.at[p], d_rs.at[slot_at], (p, 2 * z + to_core))

    @pl.when(active)
    def _():
        full[...] = part[lax.rem(z, zhalf)]

        @pl.loop(0, depth)
        def _(k):
            @pl.when(k != z)
            def _():
                send(z_send.at[0], z_recv.at[k], z_ss.at[0], z_rs.at[k],
                     (me, 2 * k + core)).wait_recv()
                full[...] += z_recv[k].astype(F32)[0:rx]

        @pl.when(to_core == core)
        def _():
            gathered[mine_at] = full[...]

        @pl.loop(0, planes)
        def _(p):
            @pl.when((p != me) | (to_core != core))
            def _():
                d_copy(p, mine_at).start()

    for u in range(units):
        @pl.when((me != 2 * u) | (core != u % 2))
        def _(u=u):
            v_copy(0, u).wait_recv()
    for u in range(units):
        cols = slice(128 * (u % 4), 128 * (u % 4) + 128)
        if u < 4:
            first_out[0:8, cols] = v_recv[u]
        else:
            first_out[8:10, cols] = v_recv[u, 0:2]
            norm_out[:, cols] = v_recv[u, 2:4]

    owner = z // zhalf
    for i in range(2):
        for y in range(SIDE):
            sender = y * SIDE + 2 * core + i

            @pl.when((sender != me) | (owner != core))
            def _(i=i, y=y):
                send(full, gathered.at[i * SIDE + y], d_ss.at[0], d_rs.at[i * SIDE + y],
                     (me, dy + 1 - 2 * core)).wait_recv()
            second_out[rx * i : rx * i + rx, 128 * y : 128 * y + 128] = gathered[i * SIDE + y]

    @pl.loop(0, units)
    def _(u):
        @pl.when((me != 2 * u) | (core != lax.rem(u, 2)))
        def _():
            send(s_send.at[u], s_recv.at[lane_of], s1_ss.at[u], s1_rs.at[lane_of],
                 (2 * u, 2 * z + lax.rem(u, 2))).wait_send()

    @pl.when(holder)
    def _():
        @pl.loop(0, depth)
        def _(k):
            @pl.when(k != z)
            def _():
                u_copy(k, z).wait_send()

        @pl.loop(0, 2 * planes)
        def _(i):
            @pl.when(i != lane_of)
            def _():
                v_copy(i, unit).wait_send()

    @pl.loop(0, zhalf)
    def _(i):
        @pl.when(core * zhalf + i != z)
        def _():
            z_copy(i, z).wait_send()

    @pl.when(active)
    def _():
        @pl.loop(0, planes)
        def _(p):
            @pl.when((p != me) | (to_core != core))
            def _():
                d_copy(p, mine_at).wait_send()


def on_device(audio, counts, cotangent, conv_first, norm_gain, norm_bias, conv_second):
    planes = lax.axis_size("dx")
    groups = lax.axis_size("dy")
    depth = groups // 2
    crops, frames, channels = cotangent.shape[1:]
    rows_all = conv_second.shape[0]
    scale = 1.0 / math.sqrt(planes * groups * crops * frames)
    zhalf = depth // 2
    hz = zhalf // 2
    half_rows = rows_all // 2
    hrows = half_rows // 2
    rx = rows_all // depth // SIDE
    rpad = -(-rx // 16) * 16
    vm = pltpu.VMEM
    dma = pltpu.SemaphoreType.DMA
    scratch = [
        vm(audio.shape, BF16), vm(cotangent.shape, BF16), vm(conv_first.shape, BF16),
        vm((channels,), F32), vm((channels,), F32), vm(conv_second.shape, BF16), dma((6,)),
        vm((640, 640), BF16), vm((8, 16, 256), F32), vm((planes, 1, 128), jnp.int32),
        vm((planes, 16, 256), BF16), vm((planes, 16, 256), BF16),
        vm((16 * crops, 256), F32), vm((16 * crops, 256), BF16),
        vm((16, 2 * channels), F32), vm((128, channels), F32),
        vm((crops, 192, 2 * channels), BF16), vm((crops, 16, 2 * channels), F32),
        vm((crops, 8, channels), F32), vm((crops, 16, 128), F32),
        vm((2, crops * frames, half_rows), BF16), vm((crops * frames, channels), BF16),
        vm((crops, frames, channels), F32), vm((crops, frames, channels), F32),
        vm((crops, 1, channels), F32), vm((frames + 8, channels), F32),
        vm((frames + 8, channels), F32),
        vm((2, hrows, channels), F32), vm((2, hrows, channels), BF16),
        vm((2, hrows, channels), BF16),
        vm((2, planes, hz * rx, 128), BF16), vm((2, planes, hz * rx, 128), BF16),
        vm((zhalf, rx, 128), F32), vm((zhalf, rpad, 128), BF16), vm((depth, rpad, 128), BF16),
        vm((rx, 128), F32), vm((8, rx, 128), F32),
        vm((16, channels), F32), vm((16, channels), F32), vm((8, channels), F32),
        vm((16, channels), F32), vm((8, 8, 128), F32), vm((2 * planes, 8, 128), F32),
        vm((8, 128), F32), vm((depth, 8, 128), F32), vm((8, 128), F32), vm((8, 8, 128), F32),
        dma((planes,)), dma((planes,)), dma((planes,)), dma((planes,)), dma((2,)), dma((2,)),
        dma((2, planes)), dma((2, planes)), dma((zhalf,)), dma((depth,)), dma((planes,)), dma((8,)),
        dma((8,)), dma((2 * planes,)), dma((depth,)), dma((depth,)), dma((2 * planes,)), dma((8,)),
    ]
    hbm = pl.BlockSpec(memory_space=pltpu.HBM)
    vmem = pl.BlockSpec(memory_space=pltpu.VMEM)
    outs = pl.pallas_call(
        functools.partial(kernel, planes, depth, scale),
        out_shape=[
            jax.ShapeDtypeStruct(conv_first.shape, F32),
            jax.ShapeDtypeStruct((2, channels), F32),
            jax.ShapeDtypeStruct((rows_all // groups, channels), F32),
        ],
        in_specs=[hbm, vmem, hbm, hbm, hbm, hbm, hbm],
        out_specs=[vmem] * 3,
        scratch_shapes=scratch,
        compiler_params=pltpu.CompilerParams(
            collective_id=0, has_side_effects=True, vmem_limit_bytes=63 * 2**20),
    )(audio, jnp.broadcast_to(counts, (1, 128)), cotangent, conv_first, norm_gain, norm_bias, conv_second)

    def place(*refs):
        ins, results, held, sems = refs[0:3], refs[3:6], refs[6:9], refs[9]
        reads = [pltpu.make_async_copy(ins[i], held[i], sems.at[i]) for i in range(3)]
        writes = [pltpu.make_async_copy(held[i], results[i], sems.at[3 + i]) for i in range(3)]
        for read in reads:
            read.start()
        for read, write in zip(reads, writes):
            read.wait()
            write.start()
        for write in writes:
            write.wait()

    return tuple(pl.pallas_call(
        place,
        out_shape=[jax.ShapeDtypeStruct(out.shape, out.dtype) for out in outs],
        in_specs=[hbm] * 3,
        out_specs=[pl.BlockSpec(memory_space=pltpu.HBM)] * 3,
        scratch_shapes=[vm(out.shape, F32) for out in outs] + [dma((6,))],
        compiler_params=pltpu.CompilerParams(vmem_limit_bytes=63 * 2**20),
    )(*outs))


def solution(mesh):
    in_specs = (P("dy", "dx", None), P("dy", "dx"), P("dy", "dx", None, None), P(), P(), P(), P())
    out_specs = (P(), P(), P("dy", None))
    return jax.shard_map(
        on_device, mesh=mesh, in_specs=in_specs, out_specs=out_specs, check_vma=False
    )
```

```python
import functools
import math

import jax
import jax.numpy as jnp
from jax import lax
from jax.experimental import pallas as pl
from jax.experimental.pallas import tpu as pltpu
from jax.sharding import PartitionSpec as P

F32 = jnp.float32
BF16 = jnp.bfloat16
MESH = pl.DeviceIdType.MESH
SIDE = 4
TN = (((0,), (0,)), ((), ()))
NT = (((1,), (1,)), ((), ()))
NN = (((1,), (0,)), ((), ()))
LOG2E = 1.4426950408889634


def dot(a, b, dims=NN):
    return lax.dot_general(a, b, dims, preferred_element_type=F32)


def pieces(value):
    high = value.astype(BF16)
    rest = value - high.astype(F32)
    mid = rest.astype(BF16)
    low = (rest - mid.astype(F32)).astype(BF16)
    return high, mid, low


def gelu_parts(value):
    cdf = 0.5 * lax.erf(value * 0.7071067811865476) + 0.5
    slope = cdf + value * (jnp.exp2(value * value * (-0.5 * LOG2E)) * 0.3989422804014327)
    return cdf, slope


def rows_of(shape):
    return lax.broadcasted_iota(jnp.int32, shape, 0)


def cols_of(shape):
    return lax.broadcasted_iota(jnp.int32, shape, 1)


def kernel(
    planes, depth, scale,
    audio_hbm, counts_ref, cot_hbm, w1_hbm, gain_hbm, bias_hbm, w2_hbm,
    first_out, norm_out, second_out,
    audio, cot, w1, gain_ref, bias_ref, w2, load_sem,
    perm, zbuf, cnt_all, crop_send, crop_recv, xf, xp, weo, wpad, waug, gw, stat, colsum,
    hid, grows, slope_e, slope_o, slope_t, hshift, dshift,
    half_sum, pair_send, pair_recv, p_send, p_recv, part, z_send, z_recv, full, gathered,
    acc_e, acc_o, acc_t, small, s_send, s_recv, u_val, u_recv, v_val, v_recv,
    cnt_ss, cnt_rs, crop_ss, crop_rs, pair_ss, pair_rs, plane_ss, plane_rs,
    z_ss, z_rs, d_ss, d_rs, s1_ss, s1_rs, s2_ss, s2_rs, s3_ss, s3_rs,
):
    me = lax.axis_index("dx")
    dy = lax.axis_index("dy")
    core = lax.rem(dy, 2)
    z = dy // 2
    px = lax.rem(me, SIDE)
    py = me // SIDE
    xs = [px] + [lax.rem(px + k, SIDE) for k in range(1, SIDE)]
    ys = [py * SIDE] + [lax.rem(py + k, SIDE) * SIDE for k in range(1, SIDE)]
    peers = [ys[k // SIDE] + xs[k % SIDE] for k in range(planes)]
    column = [2 * lax.rem(z + k, depth) + core for k in range(depth)]
    other = 2 * z + 1 - core
    pair = (me, other)
    few = planes - 1

    def hops(k):
        return min(k % SIDE, SIDE - k % SIDE) + min(k // SIDE, SIDE - k // SIDE)

    far_first = sorted(range(1, planes), key=lambda k: -hops(k))
    zhalf = depth // 2
    frames = cot_hbm.shape[2]
    channels = w2_hbm.shape[1]
    rows_all = w2_hbm.shape[0]
    half_rows = rows_all // 2
    rz = rows_all // depth
    rx = rz // SIDE
    hz = zhalf // 2
    hrows = half_rows // 2
    total_frames = 2 * frames + 1
    crops = cot_hbm.shape[1]

    def send(src, dst, ss, rs, where):
        return pltpu.make_async_remote_copy(
            src_ref=src, dst_ref=dst, send_sem=ss, recv_sem=rs,
            device_id=where, device_id_type=MESH,
        )

    loads = [
        pltpu.make_async_copy(src, dst, load_sem.at[i])
        for i, (src, dst) in enumerate(
            ((audio_hbm, audio), (w1_hbm, w1), (gain_hbm, gain_ref), (bias_hbm, bias_ref),
             (w2_hbm, w2), (cot_hbm, cot))
        )
    ]
    for load in loads:
        load.start()

    barrier = pltpu.get_barrier_semaphore()

    for k in range(planes):
        if k:
            pl.semaphore_signal(barrier, inc=1, device_id=(peers[k], dy), device_id_type=MESH)
        pl.semaphore_signal(barrier, inc=1, device_id=(peers[k], other), device_id_type=MESH)
    for k in range(1, depth):
        pl.semaphore_signal(barrier, inc=1, device_id=(me, column[k]), device_id_type=MESH)

    lane = cols_of((1, 640))
    sample = 10 * (lane % 64) + 2 * (lane // 128) + (lane % 128) // 64
    for i in range(5):
        block = rows_of((128, 640)) + 128 * i
        perm[pl.ds(128 * i, 128), :] = jnp.where(block == sample, 1.0, 0.0).astype(BF16)
    cnt_all[me] = jnp.broadcast_to(counts_ref[...], (1, 128))

    loads[0].wait()
    blocks = jnp.concatenate(
        [audio[0, :, 640 * i : 640 * i + 640].astype(F32) for i in range(4)], axis=0
    ).astype(BF16)
    sorted_blocks = dot(blocks, perm[...])
    eye = jnp.where(rows_of((10, 256)) == cols_of((10, 256)), 1.0, 0.0).astype(BF16)
    tails = dot(audio[0, :, 2560:2570], eye)
    low_lane = cols_of((8, 128)) < 64
    last_lane = cols_of((8, 256)) == 255
    for m in range(10):
        g = m // 2
        parts = []
        for half in range(2):
            a = sorted_blocks[16 * half : 16 * half + 8, 128 * g : 128 * g + 128]
            b = sorted_blocks[16 * half + 8 : 16 * half + 16, 128 * g : 128 * g + 128]
            if m % 2 == 0:
                parts.append(jnp.where(low_lane, a, pltpu.roll(b, 64, 1)))
            else:
                parts.append(jnp.where(low_lane, pltpu.roll(a, 64, 1), b))
        row = jnp.concatenate(parts, axis=1)
        zbuf[:, m, :] = row
        if m < 5:
            zbuf[:, 11 + m, :] = jnp.where(last_lane, tails[:, m : m + 1], pltpu.roll(row, 255, 1))
    zbuf[:, 10, :] = tails
    slot_rows = zbuf[...].reshape(128, 256).astype(BF16)

    waug[...] = jnp.zeros_like(waug)
    loads[1].wait()
    loads[2].wait()
    loads[3].wait()
    w1v = w1[...].astype(F32)
    weo[...] = jnp.zeros_like(weo)
    weo[0:10, 0:channels] = w1v
    weo[5:10, channels:] = w1v[0:5]
    weo[11:16, channels:] = w1v[5:10]
    wpad[...] = jnp.zeros_like(wpad)
    wpad[0:10, :] = w1v

    pl.semaphore_wait(barrier, 2 * planes - 1 + depth - 1)

    for k in range(1, planes):
        send(cnt_all.at[me], cnt_all.at[me], cnt_ss.at[0], cnt_rs.at[0], (peers[k], dy)).start()
    others = cnt_all.at[pl.ds(0, few)]
    send(others, others, cnt_ss.at[0], cnt_rs.at[0], pair).wait()

    count_rows = cnt_all[...].reshape(planes, 128)
    who = rows_of((planes, 128))
    start_me = jnp.sum(jnp.where(who < me, count_rows, 0), axis=0, keepdims=True)
    count_me = jnp.sum(jnp.where(who == me, count_rows, 0), axis=0, keepdims=True)
    shape = (16 * planes, 128)
    rr, cc = rows_of(shape), cols_of(shape)
    slot = cc // 16
    pick = (rr % 16 == cc % 16) & (slot < count_me) & ((start_me + slot) % planes == rr // 16)
    routed = dot(jnp.where(pick, 1.0, 0.0).astype(BF16), slot_rows).astype(BF16)
    crop_send[...] = routed.reshape(planes, 16, 256)

    for k in range(1, planes):
        send(crop_send.at[peers[k]], crop_recv.at[me], crop_ss.at[0], crop_rs.at[0],
             (peers[k], dy)).start()

    crop_recv[me] = crop_send[me]
    wide = jnp.concatenate([count_rows, count_rows], axis=1)
    who2, col2 = rows_of((planes, 256)), cols_of((planes, 256)) // 16
    start_col = jnp.sum(jnp.where(who2 < col2, wide, 0), axis=0, keepdims=True)
    count_col = jnp.sum(jnp.where(who2 == col2, wide, 0), axis=0, keepdims=True)
    shape = (16 * crops, 256)
    rr, cc = rows_of(shape), cols_of(shape)
    order = (rr // 16) * planes + me
    pick = (rr % 16 == cc % 16) & (start_col <= order) & (order < start_col + count_col)
    pick = jnp.where(pick, 1.0, 0.0).astype(BF16)

    send(crop_send.at[pl.ds(0, few)], crop_recv.at[pl.ds(0, few)], crop_ss.at[0], crop_rs.at[0],
         pair).wait()

    mine = dot(pick, crop_recv[...].reshape(16 * planes, 256))
    xf[...] = mine
    xp_all = jnp.where(rows_of((16 * crops, 256)) % 16 == 10, 1.0, mine)
    xp[...] = xp_all.astype(BF16)
    xt = jnp.concatenate([xp_all] * 3, axis=0).T.astype(BF16)

    tail_rows = jnp.concatenate(
        [xf[16 * r + 10 : 16 * r + 11, 0:128] for r in range(crops)]
        + [jnp.zeros((8 - crops, 128), F32)], axis=0)
    tail_pre = dot(tail_rows.astype(BF16), wpad[...].astype(BF16))
    gain = gain_ref[...].reshape(1, channels)
    bias = bias_ref[...].reshape(1, channels)
    we, wo = weo[:, 0:channels], weo[:, channels:]
    weo16 = weo[...].astype(BF16)
    row16 = rows_of((16, channels))
    for r in range(crops):
        x16 = xp[16 * r : 16 * r + 16, :]
        gram = dot(x16, x16, NT)
        g1, g2, g3 = pieces(gram)
        gwv = dot(g1, weo16) + dot(g2, weo16) + dot(g3, weo16)
        gw[r] = gwv
        colsum[r] = jnp.broadcast_to(gram[:, 10:11], (16, 128))
        pre_t = tail_pre[r : r + 1]
        gwe, gwo = gwv[:, 0:channels], gwv[:, channels:]
        mu = (gwe[10:11] + gwo[10:11] + pre_t) * (1.0 / total_frames)
        square = jnp.sum(we * gwe + wo * gwo, axis=0, keepdims=True) + pre_t * pre_t
        var = jnp.maximum(square * (1.0 / total_frames) - mu * mu, 0.0)
        inv = lax.rsqrt(var + 1e-5)
        mul = inv * gain
        add = bias - mu * mul
        stat[r, 0:1] = mu
        stat[r, 1:2] = inv
        stat[r, 2:3] = mul
        stat[r, 3:4] = pre_t
        stat[r, 4:5] = pre_t * mul + add
        for side, w in ((0, we), (1, wo)):
            scaled = jnp.where(row16 == 10, add, w * mul)
            for i, piece in enumerate(pieces(scaled)):
                waug[r, 64 * i + 16 * r : 64 * i + 16 * r + 16,
                     side * channels : (side + 1) * channels] = piece

    loads[4].wait()
    loads[5].wait()
    quarter = channels // 2
    xt_parts = [xt[128 * i : 128 * i + 128] for i in range(frames // 128)]

    for r in range(crops):
        base = pl.multiple_of(r * frames, frames)
        tail = stat[r, 4:5]
        cdf, slope = gelu_parts(tail)
        hshift[frames : frames + 1, :] = tail * cdf
        slope_t[r] = slope
        for n in range(4):
            for i in range(frames // 128):
                value = dot(xt_parts[i], waug[r, :, n * quarter : (n + 1) * quarter])
                cdf, slope = gelu_parts(value)
                value = value * cdf
                lo = (n % 2) * quarter
                if n < 2:
                    slope_e[r, 128 * i : 128 * i + 128, lo : lo + quarter] = slope
                    hshift[128 * i : 128 * i + 128, lo : lo + quarter] = value
                    hid[0, pl.ds(base + 128 * i, 128), lo : lo + quarter] = value.astype(BF16)
                else:
                    slope_o[r, 128 * i : 128 * i + 128, lo : lo + quarter] = slope
                    at = 512 if n == 2 else 0
                    hid[n - 2, pl.ds(base + 128 * i, 128), at : at + quarter] = value.astype(BF16)
        hid[1, pl.ds(base, frames), quarter:] = hshift[1 : frames + 1, :].astype(BF16)
        for n in range(2):
            cols = slice(n * quarter, (n + 1) * quarter)
            pre = dot(hid[0, pl.ds(base, frames), :], w2[0:half_rows, cols])
            pre = pre + dot(hid[1, pl.ds(base, frames), :], w2[half_rows:, cols])
            slope = gelu_parts(pre)[1]
            grad = (scale * cot[0, r, :, cols].astype(F32)) * slope
            grows[pl.ds(base, frames), cols] = grad.astype(BF16)

    for h in range(2):
        theirs = dot(hid[1 - core, :, h * hrows : (h + 1) * hrows], grows[...], TN)
        pair_send[h] = theirs.astype(BF16)
        send(pair_send.at[h], pair_recv.at[h], pair_ss.at[h], pair_rs.at[h], pair).start()
        if h == 0:
            half_sum[0] = dot(hid[core, :, 0:hrows], grows[...], TN)

    for h in range(2):
        if h == 1:
            half_sum[1] = dot(hid[core, :, hrows:], grows[...], TN)
        send(pair_send.at[h], pair_recv.at[h], pair_ss.at[h], pair_rs.at[h], pair).wait()
        half_sum[h] = half_sum[h] + pair_recv[h].astype(F32)
        for p in range(planes):
            lanes = slice(128 * (p // SIDE), 128 * (p // SIDE) + 128)
            first = (p % SIDE) * rx
            p_send[h, p] = jnp.concatenate(
                [half_sum[h, i * rz + first : i * rz + first + rx, lanes] for i in range(hz)], axis=0
            ).astype(BF16)

        p_recv[h, me] = jnp.zeros((hz * rx, 128), BF16)
        for k in far_first:
            send(p_send.at[h, peers[k]], p_recv.at[h, me], plane_ss.at[h, 0], plane_rs.at[h, 0],
                 (peers[k], dy)).start()

    acc_e[...] = jnp.zeros_like(acc_e)
    acc_o[...] = jnp.zeros_like(acc_o)
    acc_t[...] = jnp.zeros_like(acc_t)
    small[...] = jnp.zeros_like(small)
    dshift[0:8, :] = jnp.zeros((8, channels), F32)

    def backward(r):
        base = pl.multiple_of(r * frames, frames)
        grad = grows[pl.ds(base, frames), :]
        x16 = xp[pl.ds(pl.multiple_of(16 * r, 16), 16), :]
        shift_o = dot(grad, w2[channels : 2 * channels, :], NT) * slope_o[r]
        p_o = dot(x16, shift_o.astype(BF16))
        dshift[8 : 8 + frames, :] = dot(grad, w2[2 * channels :, :], NT)
        shift_e = dot(grad, w2[0:channels, :], NT) + dshift[7 : 7 + frames, :]
        p_e = dot(x16, (shift_e * slope_e[r]).astype(BF16))
        shift_t = dshift[7 + frames : 8 + frames, :] * slope_t[r]
        mu, inv, mul, pre_t = stat[r, 0:1], stat[r, 1:2], stat[r, 2:3], stat[r, 3:4]
        total = p_e[10:11] + p_o[10:11] + shift_t
        with_pre = jnp.sum(weo[:, 0:channels] * p_e + weo[:, channels:] * p_o, axis=0, keepdims=True)
        with_norm = inv * (with_pre + pre_t * shift_t - mu * total)
        small[10:11, :] = small[10:11, :] + with_norm
        small[11:12, :] = small[11:12, :] + total
        mean_g = total * (1.0 / total_frames)
        mean_n = with_norm * (1.0 / total_frames) * inv
        sums = jnp.concatenate([colsum[r]] * (channels // 128), axis=1)
        base_part = mean_g * sums
        acc_e[...] += mul * (p_e - base_part - mean_n * (gw[r, :, 0:channels] - mu * sums))
        acc_o[...] += mul * (p_o - base_part - mean_n * (gw[r, :, channels:] - mu * sums))
        acc_t[pl.ds(r, 1), :] = mul * (shift_t - mean_g - mean_n * (pre_t - mu))

    for r in range(crops):
        backward(r)

    tail_grad = lax.dot_general(
        tail_rows, acc_t[...], TN, preferred_element_type=F32, precision=lax.Precision.HIGHEST)
    small[0:10, :] = acc_e[0:10, :] + tail_grad[0:10, :]
    small[0:5, :] = small[0:5, :] + acc_o[5:10, :]
    small[5:10, :] = small[5:10, :] + acc_o[11:16, :]

    units = 8
    for u in range(units):
        s_send[u] = small[8 * (u // 4) : 8 * (u // 4) + 8, 128 * (u % 4) : 128 * (u % 4) + 128]
    lane_of = me * 2 + core
    unit = me // 2
    holder = (lax.rem(me, 2) == 0) & (core == lax.rem(unit, 2))

    for u in range(units):
        mine_u = (me == 2 * u) & (core == u % 2)

        @pl.when(mine_u)
        def _(u=u):
            s_recv[lane_of] = s_send[u]

        @pl.when(jnp.logical_not(mine_u))
        def _(u=u):
            send(s_send.at[u], s_recv.at[lane_of], s1_ss.at[0], s1_rs.at[0],
                 (2 * u, 2 * z + u % 2)).start()

    mine_rows = pl.multiple_of(px * rx, 8)
    mine_lanes = pl.ds(pl.multiple_of(128 * py, 128), 128)
    pad = z_send.shape[1] - rx

    z_recv[z] = jnp.zeros(z_recv.shape[1:], BF16)

    for h in range(2):
        own = jnp.concatenate(
            [half_sum[h, pl.ds(i * rz + mine_rows, rx), mine_lanes] for i in range(hz)], axis=0)

        send(p_send.at[h, pl.ds(0, few)], p_recv.at[h, pl.ds(0, few)], plane_ss.at[h, 0],
             plane_rs.at[h, 0], pair).wait()
        for p in range(planes):
            own = own + p_recv[h, p].astype(F32)
        own = own.reshape(hz, rx, 128)
        part[h * hz : h * hz + hz] = own
        padding = [jnp.zeros((hz, pad, 128), F32)] if pad else []
        z_send[h * hz : h * hz + hz] = jnp.concatenate([own] + padding, axis=1).astype(BF16)

        for i in range(h * hz, h * hz + hz):
            @pl.when(core * zhalf + i != z)
            def _(i=i):
                send(z_send.at[i], z_recv.at[z], z_ss.at[0], z_rs.at[0],
                     (me, 2 * (core * zhalf + i) + core)).start()

    @pl.when(holder)
    def _():
        rest = s_recv.at[pl.ds(0, 2 * planes - 1)]
        send(rest, rest, s1_ss.at[0], s1_rs.at[0], pair).wait_recv()
        total = jnp.sum(s_recv[...], axis=0)
        u_val[...] = total
        u_recv[z] = total
        for k in range(1, depth):
            send(u_val, u_recv.at[z], s2_ss.at[0], s2_rs.at[0], (me, column[k])).start()

    active = z // zhalf == core
    to_core = px // 2
    mine_at = lax.rem(px, 2) * SIDE + py

    d_to = 2 * z + to_core

    @pl.when(active)
    def _():
        rest = z_recv.at[pl.ds(0, depth - 1)]
        send(rest, rest, z_ss.at[0], z_rs.at[0], pair).wait_recv()
        total = part[lax.rem(z, zhalf)]
        for k in range(depth):
            total = total + z_recv[k].astype(F32)[0:rx]
        full[...] = total
        for k in range(1, planes):
            send(full, gathered.at[mine_at], d_ss.at[0], d_rs.at[0], (peers[k], d_to)).start()

        @pl.when(to_core == core)
        def _():
            gathered[mine_at] = full[...]

        @pl.when(to_core != core)
        def _():
            send(full, gathered.at[mine_at], d_ss.at[0], d_rs.at[0], pair).start()

    @pl.when(holder)
    def _():
        rest = u_recv.at[pl.ds(0, depth - 1)]
        send(rest, rest, s2_ss.at[0], s2_rs.at[0], pair).wait()
        total = jnp.sum(u_recv[...], axis=0)
        v_val[...] = total
        v_recv[unit] = total
        for k in range(planes):
            if k:
                send(v_val, v_recv.at[unit], s3_ss.at[0], s3_rs.at[0], (peers[k], dy)).start()
            send(v_val, v_recv.at[unit], s3_ss.at[0], s3_rs.at[0], (peers[k], other)).start()
        rest = v_recv.at[pl.ds(0, units - 1)]
        send(rest, rest, s3_ss.at[0], s3_rs.at[0], pair).wait_recv()
        sent = s_send.at[pl.ds(0, units - 1)]
        send(sent, sent, s1_ss.at[0], s1_rs.at[0], pair).wait_send()

    @pl.when(jnp.logical_not(holder))
    def _():
        send(v_recv, v_recv, s3_ss.at[0], s3_rs.at[0], pair).wait_recv()
        send(s_send, s_send, s1_ss.at[0], s1_rs.at[0], pair).wait_send()

    for u in range(units):
        cols = slice(128 * (u % 4), 128 * (u % 4) + 128)
        if u < 4:
            first_out[0:8, cols] = v_recv[u]
        else:
            first_out[8:10, cols] = v_recv[u, 0:2]
            norm_out[:, cols] = v_recv[u, 2:4]

    lands_here = active & (to_core == core)

    @pl.when(lands_here)
    def _():
        rest = gathered.at[pl.ds(0, 2 * SIDE - 1)]
        send(rest, rest, d_ss.at[0], d_rs.at[0], pair).wait_recv()

    @pl.when(jnp.logical_not(lands_here))
    def _():
        rest = gathered.at[pl.ds(0, 2 * SIDE)]
        send(rest, rest, d_ss.at[0], d_rs.at[0], pair).wait_recv()

    for i in range(2):
        for y in range(SIDE):
            second_out[rx * i : rx * i + rx, 128 * y : 128 * y + 128] = gathered[i * SIDE + y]

    @pl.when(holder)
    def _():
        sent = s_recv.at[pl.ds(0, 2 * planes - 1)]
        send(sent, sent, s3_ss.at[0], s3_rs.at[0], pair).wait_send()

    @pl.when(active)
    def _():
        sent = z_send.at[pl.ds(0, zhalf - 1)]
        send(sent, sent, z_ss.at[0], z_rs.at[0], pair).wait_send()

        @pl.when(to_core == core)
        def _():
            sent = gathered.at[pl.ds(0, planes - 1)]
            send(sent, sent, d_ss.at[0], d_rs.at[0], pair).wait_send()

        @pl.when(to_core != core)
        def _():
            send(gathered, gathered, d_ss.at[0], d_rs.at[0], pair).wait_send()

    @pl.when(jnp.logical_not(active))
    def _():
        send(z_send, z_send, z_ss.at[0], z_rs.at[0], pair).wait_send()


def on_device(audio, counts, cotangent, conv_first, norm_gain, norm_bias, conv_second):
    planes = lax.axis_size("dx")
    groups = lax.axis_size("dy")
    depth = groups // 2
    crops, frames, channels = cotangent.shape[1:]
    rows_all = conv_second.shape[0]
    scale = 1.0 / math.sqrt(planes * groups * crops * frames)
    zhalf = depth // 2
    hz = zhalf // 2
    half_rows = rows_all // 2
    hrows = half_rows // 2
    rx = rows_all // depth // SIDE
    rpad = -(-rx // 16) * 16
    vm = pltpu.VMEM
    dma = pltpu.SemaphoreType.DMA
    scratch = [
        vm(audio.shape, BF16), vm(cotangent.shape, BF16), vm(conv_first.shape, BF16),
        vm((channels,), F32), vm((channels,), F32), vm(conv_second.shape, BF16), dma((6,)),
        vm((640, 640), BF16), vm((8, 16, 256), F32), vm((planes, 1, 128), jnp.int32),
        vm((planes, 16, 256), BF16), vm((planes, 16, 256), BF16),
        vm((16 * crops, 256), F32), vm((16 * crops, 256), BF16),
        vm((16, 2 * channels), F32), vm((128, channels), F32),
        vm((crops, 192, 2 * channels), BF16), vm((crops, 16, 2 * channels), F32),
        vm((crops, 8, channels), F32), vm((crops, 16, 128), F32),
        vm((2, crops * frames, half_rows), BF16), vm((crops * frames, channels), BF16),
        vm((crops, frames, channels), F32), vm((crops, frames, channels), F32),
        vm((crops, 1, channels), F32), vm((frames + 8, channels), F32),
        vm((frames + 8, channels), F32),
        vm((2, hrows, channels), F32), vm((2, hrows, channels), BF16),
        vm((2, hrows, channels), BF16),
        vm((2, planes, hz * rx, 128), BF16), vm((2, planes, hz * rx, 128), BF16),
        vm((zhalf, rx, 128), F32), vm((zhalf, rpad, 128), BF16), vm((depth, rpad, 128), BF16),
        vm((rx, 128), F32), vm((planes, rx, 128), F32),
        vm((16, channels), F32), vm((16, channels), F32), vm((8, channels), F32),
        vm((16, channels), F32), vm((8, 8, 128), F32), vm((2 * planes, 8, 128), F32),
        vm((8, 128), F32), vm((depth, 8, 128), F32), vm((8, 128), F32), vm((8, 8, 128), F32),
        dma((planes,)), dma((planes,)), dma((planes,)), dma((planes,)), dma((2,)), dma((2,)),
        dma((2, planes)), dma((2, planes)), dma((zhalf,)), dma((depth,)), dma((planes,)), dma((8,)),
        dma((8,)), dma((2 * planes,)), dma((depth,)), dma((depth,)), dma((2 * planes,)), dma((8,)),
    ]
    hbm = pl.BlockSpec(memory_space=pltpu.HBM)
    vmem = pl.BlockSpec(memory_space=pltpu.VMEM)
    outs = pl.pallas_call(
        functools.partial(kernel, planes, depth, scale),
        out_shape=[
            jax.ShapeDtypeStruct(conv_first.shape, F32),
            jax.ShapeDtypeStruct((2, channels), F32),
            jax.ShapeDtypeStruct((rows_all // groups, channels), F32),
        ],
        in_specs=[hbm, vmem, hbm, hbm, hbm, hbm, hbm],
        out_specs=[vmem] * 3,
        scratch_shapes=scratch,
        compiler_params=pltpu.CompilerParams(
            collective_id=0, has_side_effects=True, vmem_limit_bytes=63 * 2**20),
    )(audio, counts, cotangent, conv_first, norm_gain, norm_bias, conv_second)

    def place(*refs):
        ins, results, held, sems = refs[0:3], refs[3:6], refs[6:9], refs[9]
        reads = [pltpu.make_async_copy(ins[i], held[i], sems.at[i]) for i in range(3)]
        writes = [pltpu.make_async_copy(held[i], results[i], sems.at[3 + i]) for i in range(3)]
        for read in reads:
            read.start()
        for read, write in zip(reads, writes):
            read.wait()
            write.start()
        for write in writes:
            write.wait()

    return tuple(pl.pallas_call(
        place,
        out_shape=[jax.ShapeDtypeStruct(out.shape, out.dtype) for out in outs],
        in_specs=[hbm] * 3,
        out_specs=[pl.BlockSpec(memory_space=pltpu.HBM)] * 3,
        scratch_shapes=[vm(out.shape, F32) for out in outs] + [dma((6,))],
        compiler_params=pltpu.CompilerParams(vmem_limit_bytes=63 * 2**20),
    )(*outs))


def solution(mesh):
    in_specs = (P("dy", "dx", None), P("dy", "dx"), P("dy", "dx", None, None), P(), P(), P(), P())
    out_specs = (P(), P(), P("dy", None))
    return jax.shard_map(
        on_device, mesh=mesh, in_specs=in_specs, out_specs=out_specs, check_vma=False
    )
```

```python
import functools
import math

import jax
import jax.numpy as jnp
from jax import lax
from jax.experimental import pallas as pl
from jax.experimental.pallas import tpu as pltpu
from jax.sharding import PartitionSpec as P

F32 = jnp.float32
BF16 = jnp.bfloat16
MESH = pl.DeviceIdType.MESH
SIDE = 4
TN = (((0,), (0,)), ((), ()))
NT = (((1,), (1,)), ((), ()))
NN = (((1,), (0,)), ((), ()))
LOG2E = 1.4426950408889634


def dot(a, b, dims=NN):
    return lax.dot_general(a, b, dims, preferred_element_type=F32)


def pieces(value):
    high = value.astype(BF16)
    rest = value - high.astype(F32)
    mid = rest.astype(BF16)
    low = (rest - mid.astype(F32)).astype(BF16)
    return high, mid, low


def gelu_parts(value):
    cdf = 0.5 * lax.erf(value * 0.7071067811865476) + 0.5
    slope = cdf + value * (jnp.exp2(value * value * (-0.5 * LOG2E)) * 0.3989422804014327)
    return cdf, slope


def rows_of(shape):
    return lax.broadcasted_iota(jnp.int32, shape, 0)


def cols_of(shape):
    return lax.broadcasted_iota(jnp.int32, shape, 1)


def kernel(
    planes, depth, scale,
    audio_hbm, counts_ref, cot_hbm, w1_hbm, gain_hbm, bias_hbm, w2_hbm,
    first_out, norm_out, second_out,
    audio, cot, w1, gain_ref, bias_ref, w2, load_sem,
    perm, zbuf, cnt_all, crop_send, crop_recv, xf, xp, weo, wpad, waug, gw, stat, colsum,
    hid, grows, slope_e, slope_o, slope_t, hshift, dshift,
    half_sum, pair_send, pair_recv, p_send, p_recv, part, z_send, z_recv, full, gathered,
    acc_e, acc_o, acc_t, small, s_send, s_recv, u_val, u_recv, v_val, v_recv,
    cnt_ss, cnt_rs, crop_ss, crop_rs, pair_ss, pair_rs, plane_ss, plane_rs,
    z_ss, z_rs, d_ss, d_rs, s1_ss, s1_rs, s2_ss, s2_rs, s3_ss, s3_rs,
    from_below, from_above,
):
    me = lax.axis_index("dx")
    dy = lax.axis_index("dy")
    core = lax.rem(dy, 2)
    z = dy // 2
    px = lax.rem(me, SIDE)
    py = me // SIDE
    xs = [px] + [lax.rem(px + k, SIDE) for k in range(1, SIDE)]
    ys = [py * SIDE] + [lax.rem(py + k, SIDE) * SIDE for k in range(1, SIDE)]
    peers = [ys[k // SIDE] + xs[k % SIDE] for k in range(planes)]
    column = [2 * lax.rem(z + k, depth) + core for k in range(depth)]
    other = 2 * z + 1 - core
    pair = (me, other)
    few = planes - 1

    def hops(k):
        return min(k % SIDE, SIDE - k % SIDE) + min(k // SIDE, SIDE - k // SIDE)

    far_first = sorted(range(1, planes), key=lambda k: -hops(k))
    zhalf = depth // 2
    frames = cot_hbm.shape[2]
    channels = w2_hbm.shape[1]
    rows_all = w2_hbm.shape[0]
    half_rows = rows_all // 2
    rz = rows_all // depth
    rx = rz // SIDE
    hz = zhalf // 2
    hrows = half_rows // 2
    total_frames = 2 * frames + 1
    crops = cot_hbm.shape[1]

    def send(src, dst, ss, rs, where):
        return pltpu.make_async_remote_copy(
            src_ref=src, dst_ref=dst, send_sem=ss, recv_sem=rs,
            device_id=where, device_id_type=MESH,
        )

    loads = [
        pltpu.make_async_copy(src, dst, load_sem.at[i])
        for i, (src, dst) in enumerate(
            ((audio_hbm, audio), (w1_hbm, w1), (gain_hbm, gain_ref), (bias_hbm, bias_ref),
             (w2_hbm, w2), (cot_hbm, cot))
        )
    ]
    for load in loads:
        load.start()

    barrier = pltpu.get_barrier_semaphore()

    for k in range(planes):
        if k:
            pl.semaphore_signal(barrier, inc=1, device_id=(peers[k], dy), device_id_type=MESH)
        pl.semaphore_signal(barrier, inc=1, device_id=(peers[k], other), device_id_type=MESH)
    for k in (1, depth - 1):
        pl.semaphore_signal(barrier, inc=1, device_id=(me, column[k]), device_id_type=MESH)
    rounds = depth // 2 - 1

    def tell(j):
        if j <= rounds:
            pl.semaphore_signal(from_below.at[j - 1], inc=1, device_id=(me, column[1]), device_id_type=MESH)
            pl.semaphore_signal(from_above.at[j - 1], inc=1, device_id=(me, column[depth - 1]), device_id_type=MESH)

    def hear(j):
        if j <= rounds:
            pl.semaphore_wait(from_below.at[j - 1], 1)
            pl.semaphore_wait(from_above.at[j - 1], 1)

    lane = cols_of((1, 640))
    sample = 10 * (lane % 64) + 2 * (lane // 128) + (lane % 128) // 64
    for i in range(5):
        block = rows_of((128, 640)) + 128 * i
        perm[pl.ds(128 * i, 128), :] = jnp.where(block == sample, 1.0, 0.0).astype(BF16)
    cnt_all[me] = jnp.broadcast_to(counts_ref[...], (1, 128))

    loads[0].wait()
    blocks = jnp.concatenate(
        [audio[0, :, 640 * i : 640 * i + 640].astype(F32) for i in range(4)], axis=0
    ).astype(BF16)
    sorted_blocks = dot(blocks, perm[...])
    eye = jnp.where(rows_of((10, 256)) == cols_of((10, 256)), 1.0, 0.0).astype(BF16)
    tails = dot(audio[0, :, 2560:2570], eye)
    low_lane = cols_of((8, 128)) < 64
    last_lane = cols_of((8, 256)) == 255
    for m in range(10):
        g = m // 2
        parts = []
        for half in range(2):
            a = sorted_blocks[16 * half : 16 * half + 8, 128 * g : 128 * g + 128]
            b = sorted_blocks[16 * half + 8 : 16 * half + 16, 128 * g : 128 * g + 128]
            if m % 2 == 0:
                parts.append(jnp.where(low_lane, a, pltpu.roll(b, 64, 1)))
            else:
                parts.append(jnp.where(low_lane, pltpu.roll(a, 64, 1), b))
        row = jnp.concatenate(parts, axis=1)
        zbuf[:, m, :] = row
        if m < 5:
            zbuf[:, 11 + m, :] = jnp.where(last_lane, tails[:, m : m + 1], pltpu.roll(row, 255, 1))
    zbuf[:, 10, :] = tails
    slot_rows = zbuf[...].reshape(128, 256).astype(BF16)

    waug[...] = jnp.zeros_like(waug)
    loads[1].wait()
    loads[2].wait()
    loads[3].wait()
    w1v = w1[...].astype(F32)
    weo[...] = jnp.zeros_like(weo)
    weo[0:10, 0:channels] = w1v
    weo[5:10, channels:] = w1v[0:5]
    weo[11:16, channels:] = w1v[5:10]
    wpad[...] = jnp.zeros_like(wpad)
    wpad[0:10, :] = w1v

    pl.semaphore_wait(barrier, 2 * planes - 1 + 2)
    tell(1)

    for k in range(1, planes):
        send(cnt_all.at[me], cnt_all.at[me], cnt_ss.at[0], cnt_rs.at[0], (peers[k], dy)).start()
    others = cnt_all.at[pl.ds(0, few)]
    send(others, others, cnt_ss.at[0], cnt_rs.at[0], pair).wait()

    hear(1)
    tell(2)
    count_rows = cnt_all[...].reshape(planes, 128)
    who = rows_of((planes, 128))
    start_me = jnp.sum(jnp.where(who < me, count_rows, 0), axis=0, keepdims=True)
    count_me = jnp.sum(jnp.where(who == me, count_rows, 0), axis=0, keepdims=True)
    shape = (16 * planes, 128)
    rr, cc = rows_of(shape), cols_of(shape)
    slot = cc // 16
    pick = (rr % 16 == cc % 16) & (slot < count_me) & ((start_me + slot) % planes == rr // 16)
    routed = dot(jnp.where(pick, 1.0, 0.0).astype(BF16), slot_rows).astype(BF16)
    crop_send[...] = routed.reshape(planes, 16, 256)

    for k in range(1, planes):
        send(crop_send.at[peers[k]], crop_recv.at[me], crop_ss.at[0], crop_rs.at[0],
             (peers[k], dy)).start()

    crop_recv[me] = crop_send[me]
    wide = jnp.concatenate([count_rows, count_rows], axis=1)
    who2, col2 = rows_of((planes, 256)), cols_of((planes, 256)) // 16
    start_col = jnp.sum(jnp.where(who2 < col2, wide, 0), axis=0, keepdims=True)
    count_col = jnp.sum(jnp.where(who2 == col2, wide, 0), axis=0, keepdims=True)
    shape = (16 * crops, 256)
    rr, cc = rows_of(shape), cols_of(shape)
    order = (rr // 16) * planes + me
    pick = (rr % 16 == cc % 16) & (start_col <= order) & (order < start_col + count_col)
    pick = jnp.where(pick, 1.0, 0.0).astype(BF16)

    send(crop_send.at[pl.ds(0, few)], crop_recv.at[pl.ds(0, few)], crop_ss.at[0], crop_rs.at[0],
         pair).wait()

    hear(2)
    tell(3)
    mine = dot(pick, crop_recv[...].reshape(16 * planes, 256))
    xf[...] = mine
    xp_all = jnp.where(rows_of((16 * crops, 256)) % 16 == 10, 1.0, mine)
    xp[...] = xp_all.astype(BF16)
    xt = jnp.concatenate([xp_all] * 3, axis=0).T.astype(BF16)

    tail_rows = jnp.concatenate(
        [xf[16 * r + 10 : 16 * r + 11, 0:128] for r in range(crops)]
        + [jnp.zeros((8 - crops, 128), F32)], axis=0)
    tail_pre = dot(tail_rows.astype(BF16), wpad[...].astype(BF16))
    gain = gain_ref[...].reshape(1, channels)
    bias = bias_ref[...].reshape(1, channels)
    we, wo = weo[:, 0:channels], weo[:, channels:]
    weo16 = weo[...].astype(BF16)
    row16 = rows_of((16, channels))
    for r in range(crops):
        x16 = xp[16 * r : 16 * r + 16, :]
        gram = dot(x16, x16, NT)
        g1, g2, g3 = pieces(gram)
        gwv = dot(g1, weo16) + dot(g2, weo16) + dot(g3, weo16)
        gw[r] = gwv
        colsum[r] = jnp.broadcast_to(gram[:, 10:11], (16, 128))
        pre_t = tail_pre[r : r + 1]
        gwe, gwo = gwv[:, 0:channels], gwv[:, channels:]
        mu = (gwe[10:11] + gwo[10:11] + pre_t) * (1.0 / total_frames)
        square = jnp.sum(we * gwe + wo * gwo, axis=0, keepdims=True) + pre_t * pre_t
        var = jnp.maximum(square * (1.0 / total_frames) - mu * mu, 0.0)
        inv = lax.rsqrt(var + 1e-5)
        mul = inv * gain
        add = bias - mu * mul
        stat[r, 0:1] = mu
        stat[r, 1:2] = inv
        stat[r, 2:3] = mul
        stat[r, 3:4] = pre_t
        stat[r, 4:5] = pre_t * mul + add
        for side, w in ((0, we), (1, wo)):
            scaled = jnp.where(row16 == 10, add, w * mul)
            for i, piece in enumerate(pieces(scaled)):
                waug[r, 64 * i + 16 * r : 64 * i + 16 * r + 16,
                     side * channels : (side + 1) * channels] = piece

    hear(3)
    tell(4)
    loads[4].wait()
    loads[5].wait()
    quarter = channels // 2
    xt_parts = [xt[128 * i : 128 * i + 128] for i in range(frames // 128)]

    for r in range(crops):
        base = pl.multiple_of(r * frames, frames)
        tail = stat[r, 4:5]
        cdf, slope = gelu_parts(tail)
        hshift[frames : frames + 1, :] = tail * cdf
        slope_t[r] = slope
        for n in range(4):
            for i in range(frames // 128):
                value = dot(xt_parts[i], waug[r, :, n * quarter : (n + 1) * quarter])
                cdf, slope = gelu_parts(value)
                value = value * cdf
                lo = (n % 2) * quarter
                if n < 2:
                    slope_e[r, 128 * i : 128 * i + 128, lo : lo + quarter] = slope
                    hshift[128 * i : 128 * i + 128, lo : lo + quarter] = value
                    hid[0, pl.ds(base + 128 * i, 128), lo : lo + quarter] = value.astype(BF16)
                else:
                    slope_o[r, 128 * i : 128 * i + 128, lo : lo + quarter] = slope
                    at = 512 if n == 2 else 0
                    hid[n - 2, pl.ds(base + 128 * i, 128), at : at + quarter] = value.astype(BF16)
        hid[1, pl.ds(base, frames), quarter:] = hshift[1 : frames + 1, :].astype(BF16)
        for n in range(2):
            cols = slice(n * quarter, (n + 1) * quarter)
            pre = dot(hid[0, pl.ds(base, frames), :], w2[0:half_rows, cols])
            pre = pre + dot(hid[1, pl.ds(base, frames), :], w2[half_rows:, cols])
            slope = gelu_parts(pre)[1]
            grad = (scale * cot[0, r, :, cols].astype(F32)) * slope
            grows[pl.ds(base, frames), cols] = grad.astype(BF16)
        hear(r + 4)
        tell(r + 5)

    for h in range(2):
        theirs = dot(hid[1 - core, :, h * hrows : (h + 1) * hrows], grows[...], TN)
        pair_send[h] = theirs.astype(BF16)
        send(pair_send.at[h], pair_recv.at[h], pair_ss.at[h], pair_rs.at[h], pair).start()
        if h == 0:
            half_sum[0] = dot(hid[core, :, 0:hrows], grows[...], TN)

    for h in range(2):
        if h == 1:
            half_sum[1] = dot(hid[core, :, hrows:], grows[...], TN)
        send(pair_send.at[h], pair_recv.at[h], pair_ss.at[h], pair_rs.at[h], pair).wait()
        half_sum[h] = half_sum[h] + pair_recv[h].astype(F32)
        for p in range(planes):
            lanes = slice(128 * (p // SIDE), 128 * (p // SIDE) + 128)
            first = (p % SIDE) * rx
            p_send[h, p] = jnp.concatenate(
                [half_sum[h, i * rz + first : i * rz + first + rx, lanes] for i in range(hz)], axis=0
            ).astype(BF16)

        p_recv[h, me] = jnp.zeros((hz * rx, 128), BF16)
        for k in far_first:
            send(p_send.at[h, peers[k]], p_recv.at[h, me], plane_ss.at[h, 0], plane_rs.at[h, 0],
                 (peers[k], dy)).start()

    acc_e[...] = jnp.zeros_like(acc_e)
    acc_o[...] = jnp.zeros_like(acc_o)
    acc_t[...] = jnp.zeros_like(acc_t)
    small[...] = jnp.zeros_like(small)
    dshift[0:8, :] = jnp.zeros((8, channels), F32)

    def backward(r):
        base = pl.multiple_of(r * frames, frames)
        grad = grows[pl.ds(base, frames), :]
        x16 = xp[pl.ds(pl.multiple_of(16 * r, 16), 16), :]
        shift_o = dot(grad, w2[channels : 2 * channels, :], NT) * slope_o[r]
        p_o = dot(x16, shift_o.astype(BF16))
        dshift[8 : 8 + frames, :] = dot(grad, w2[2 * channels :, :], NT)
        shift_e = dot(grad, w2[0:channels, :], NT) + dshift[7 : 7 + frames, :]
        p_e = dot(x16, (shift_e * slope_e[r]).astype(BF16))
        shift_t = dshift[7 + frames : 8 + frames, :] * slope_t[r]
        mu, inv, mul, pre_t = stat[r, 0:1], stat[r, 1:2], stat[r, 2:3], stat[r, 3:4]
        total = p_e[10:11] + p_o[10:11] + shift_t
        with_pre = jnp.sum(weo[:, 0:channels] * p_e + weo[:, channels:] * p_o, axis=0, keepdims=True)
        with_norm = inv * (with_pre + pre_t * shift_t - mu * total)
        small[10:11, :] = small[10:11, :] + with_norm
        small[11:12, :] = small[11:12, :] + total
        mean_g = total * (1.0 / total_frames)
        mean_n = with_norm * (1.0 / total_frames) * inv
        sums = jnp.concatenate([colsum[r]] * (channels // 128), axis=1)
        base_part = mean_g * sums
        acc_e[...] += mul * (p_e - base_part - mean_n * (gw[r, :, 0:channels] - mu * sums))
        acc_o[...] += mul * (p_o - base_part - mean_n * (gw[r, :, channels:] - mu * sums))
        acc_t[pl.ds(r, 1), :] = mul * (shift_t - mean_g - mean_n * (pre_t - mu))

    for r in range(crops):
        backward(r)

    tail_grad = lax.dot_general(
        tail_rows, acc_t[...], TN, preferred_element_type=F32, precision=lax.Precision.HIGHEST)
    small[0:10, :] = acc_e[0:10, :] + tail_grad[0:10, :]
    small[0:5, :] = small[0:5, :] + acc_o[5:10, :]
    small[5:10, :] = small[5:10, :] + acc_o[11:16, :]

    units = 8
    for u in range(units):
        s_send[u] = small[8 * (u // 4) : 8 * (u // 4) + 8, 128 * (u % 4) : 128 * (u % 4) + 128]
    lane_of = me * 2 + core
    unit = me // 2
    holder = (lax.rem(me, 2) == 0) & (core == lax.rem(unit, 2))

    for u in range(units):
        mine_u = (me == 2 * u) & (core == u % 2)

        @pl.when(mine_u)
        def _(u=u):
            s_recv[lane_of] = s_send[u]

        @pl.when(jnp.logical_not(mine_u))
        def _(u=u):
            send(s_send.at[u], s_recv.at[lane_of], s1_ss.at[0], s1_rs.at[0],
                 (2 * u, 2 * z + u % 2)).start()

    mine_rows = pl.multiple_of(px * rx, 8)
    mine_lanes = pl.ds(pl.multiple_of(128 * py, 128), 128)
    pad = z_send.shape[1] - rx

    z_recv[z] = jnp.zeros(z_recv.shape[1:], BF16)

    for h in range(2):
        own = jnp.concatenate(
            [half_sum[h, pl.ds(i * rz + mine_rows, rx), mine_lanes] for i in range(hz)], axis=0)

        send(p_send.at[h, pl.ds(0, few)], p_recv.at[h, pl.ds(0, few)], plane_ss.at[h, 0],
             plane_rs.at[h, 0], pair).wait()
        for p in range(planes):
            own = own + p_recv[h, p].astype(F32)
        own = own.reshape(hz, rx, 128)
        part[h * hz : h * hz + hz] = own
        padding = [jnp.zeros((hz, pad, 128), F32)] if pad else []
        z_send[h * hz : h * hz + hz] = jnp.concatenate([own] + padding, axis=1).astype(BF16)

        for i in range(h * hz, h * hz + hz):
            @pl.when(core * zhalf + i != z)
            def _(i=i):
                send(z_send.at[i], z_recv.at[z], z_ss.at[0], z_rs.at[0],
                     (me, 2 * (core * zhalf + i) + core)).start()

    @pl.when(holder)
    def _():
        rest = s_recv.at[pl.ds(0, 2 * planes - 1)]
        send(rest, rest, s1_ss.at[0], s1_rs.at[0], pair).wait_recv()
        total = jnp.sum(s_recv[...], axis=0)
        u_val[...] = total
        u_recv[z] = total
        for k in range(1, depth):
            send(u_val, u_recv.at[z], s2_ss.at[0], s2_rs.at[0], (me, column[k])).start()

    active = z // zhalf == core
    to_core = px // 2
    mine_at = lax.rem(px, 2) * SIDE + py

    d_to = 2 * z + to_core

    @pl.when(active)
    def _():
        rest = z_recv.at[pl.ds(0, depth - 1)]
        send(rest, rest, z_ss.at[0], z_rs.at[0], pair).wait_recv()
        total = part[lax.rem(z, zhalf)]
        for k in range(depth):
            total = total + z_recv[k].astype(F32)[0:rx]
        full[...] = total
        for k in range(1, planes):
            send(full, gathered.at[mine_at], d_ss.at[0], d_rs.at[0], (peers[k], d_to)).start()

        @pl.when(to_core == core)
        def _():
            gathered[mine_at] = full[...]

        @pl.when(to_core != core)
        def _():
            send(full, gathered.at[mine_at], d_ss.at[0], d_rs.at[0], pair).start()

    @pl.when(holder)
    def _():
        rest = u_recv.at[pl.ds(0, depth - 1)]
        send(rest, rest, s2_ss.at[0], s2_rs.at[0], pair).wait()
        total = jnp.sum(u_recv[...], axis=0)
        v_val[...] = total
        v_recv[unit] = total
        for k in range(planes):
            if k:
                send(v_val, v_recv.at[unit], s3_ss.at[0], s3_rs.at[0], (peers[k], dy)).start()
            send(v_val, v_recv.at[unit], s3_ss.at[0], s3_rs.at[0], (peers[k], other)).start()
        rest = v_recv.at[pl.ds(0, units - 1)]
        send(rest, rest, s3_ss.at[0], s3_rs.at[0], pair).wait_recv()
        sent = s_send.at[pl.ds(0, units - 1)]
        send(sent, sent, s1_ss.at[0], s1_rs.at[0], pair).wait_send()

    @pl.when(jnp.logical_not(holder))
    def _():
        send(v_recv, v_recv, s3_ss.at[0], s3_rs.at[0], pair).wait_recv()
        send(s_send, s_send, s1_ss.at[0], s1_rs.at[0], pair).wait_send()

    for u in range(units):
        cols = slice(128 * (u % 4), 128 * (u % 4) + 128)
        if u < 4:
            first_out[0:8, cols] = v_recv[u]
        else:
            first_out[8:10, cols] = v_recv[u, 0:2]
            norm_out[:, cols] = v_recv[u, 2:4]

    lands_here = active & (to_core == core)

    @pl.when(lands_here)
    def _():
        rest = gathered.at[pl.ds(0, 2 * SIDE - 1)]
        send(rest, rest, d_ss.at[0], d_rs.at[0], pair).wait_recv()

    @pl.when(jnp.logical_not(lands_here))
    def _():
        rest = gathered.at[pl.ds(0, 2 * SIDE)]
        send(rest, rest, d_ss.at[0], d_rs.at[0], pair).wait_recv()

    for i in range(2):
        for y in range(SIDE):
            second_out[rx * i : rx * i + rx, 128 * y : 128 * y + 128] = gathered[i * SIDE + y]

    @pl.when(holder)
    def _():
        sent = s_recv.at[pl.ds(0, 2 * planes - 1)]
        send(sent, sent, s3_ss.at[0], s3_rs.at[0], pair).wait_send()

    @pl.when(active)
    def _():
        sent = z_send.at[pl.ds(0, zhalf - 1)]
        send(sent, sent, z_ss.at[0], z_rs.at[0], pair).wait_send()

        @pl.when(to_core == core)
        def _():
            sent = gathered.at[pl.ds(0, planes - 1)]
            send(sent, sent, d_ss.at[0], d_rs.at[0], pair).wait_send()

        @pl.when(to_core != core)
        def _():
            send(gathered, gathered, d_ss.at[0], d_rs.at[0], pair).wait_send()

    @pl.when(jnp.logical_not(active))
    def _():
        send(z_send, z_send, z_ss.at[0], z_rs.at[0], pair).wait_send()


def on_device(audio, counts, cotangent, conv_first, norm_gain, norm_bias, conv_second):
    planes = lax.axis_size("dx")
    groups = lax.axis_size("dy")
    depth = groups // 2
    crops, frames, channels = cotangent.shape[1:]
    rows_all = conv_second.shape[0]
    scale = 1.0 / math.sqrt(planes * groups * crops * frames)
    zhalf = depth // 2
    hz = zhalf // 2
    half_rows = rows_all // 2
    hrows = half_rows // 2
    rx = rows_all // depth // SIDE
    rpad = -(-rx // 16) * 16
    vm = pltpu.VMEM
    dma = pltpu.SemaphoreType.DMA
    scratch = [
        vm(audio.shape, BF16), vm(cotangent.shape, BF16), vm(conv_first.shape, BF16),
        vm((channels,), F32), vm((channels,), F32), vm(conv_second.shape, BF16), dma((6,)),
        vm((640, 640), BF16), vm((8, 16, 256), F32), vm((planes, 1, 128), jnp.int32),
        vm((planes, 16, 256), BF16), vm((planes, 16, 256), BF16),
        vm((16 * crops, 256), F32), vm((16 * crops, 256), BF16),
        vm((16, 2 * channels), F32), vm((128, channels), F32),
        vm((crops, 192, 2 * channels), BF16), vm((crops, 16, 2 * channels), F32),
        vm((crops, 8, channels), F32), vm((crops, 16, 128), F32),
        vm((2, crops * frames, half_rows), BF16), vm((crops * frames, channels), BF16),
        vm((crops, frames, channels), F32), vm((crops, frames, channels), F32),
        vm((crops, 1, channels), F32), vm((frames + 8, channels), F32),
        vm((frames + 8, channels), F32),
        vm((2, hrows, channels), F32), vm((2, hrows, channels), BF16),
        vm((2, hrows, channels), BF16),
        vm((2, planes, hz * rx, 128), BF16), vm((2, planes, hz * rx, 128), BF16),
        vm((zhalf, rx, 128), F32), vm((zhalf, rpad, 128), BF16), vm((depth, rpad, 128), BF16),
        vm((rx, 128), F32), vm((planes, rx, 128), F32),
        vm((16, channels), F32), vm((16, channels), F32), vm((8, channels), F32),
        vm((16, channels), F32), vm((8, 8, 128), F32), vm((2 * planes, 8, 128), F32),
        vm((8, 128), F32), vm((depth, 8, 128), F32), vm((8, 128), F32), vm((8, 8, 128), F32),
        dma((planes,)), dma((planes,)), dma((planes,)), dma((planes,)), dma((2,)), dma((2,)),
        dma((2, planes)), dma((2, planes)), dma((zhalf,)), dma((depth,)), dma((planes,)), dma((8,)),
        dma((8,)), dma((2 * planes,)), dma((depth,)), dma((depth,)), dma((2 * planes,)), dma((8,)),
        pltpu.SemaphoreType.REGULAR((8,)), pltpu.SemaphoreType.REGULAR((8,)),
    ]
    hbm = pl.BlockSpec(memory_space=pltpu.HBM)
    vmem = pl.BlockSpec(memory_space=pltpu.VMEM)
    outs = pl.pallas_call(
        functools.partial(kernel, planes, depth, scale),
        out_shape=[
            jax.ShapeDtypeStruct(conv_first.shape, F32),
            jax.ShapeDtypeStruct((2, channels), F32),
            jax.ShapeDtypeStruct((rows_all // groups, channels), F32),
        ],
        in_specs=[hbm, vmem, hbm, hbm, hbm, hbm, hbm],
        out_specs=[vmem] * 3,
        scratch_shapes=scratch,
        compiler_params=pltpu.CompilerParams(
            collective_id=0, has_side_effects=True, vmem_limit_bytes=63 * 2**20),
    )(audio, counts, cotangent, conv_first, norm_gain, norm_bias, conv_second)

    def place(*refs):
        ins, results, held, sems = refs[0:3], refs[3:6], refs[6:9], refs[9]
        reads = [pltpu.make_async_copy(ins[i], held[i], sems.at[i]) for i in range(3)]
        writes = [pltpu.make_async_copy(held[i], results[i], sems.at[3 + i]) for i in range(3)]
        for read in reads:
            read.start()
        for read, write in zip(reads, writes):
            read.wait()
            write.start()
        for write in writes:
            write.wait()

    return tuple(pl.pallas_call(
        place,
        out_shape=[jax.ShapeDtypeStruct(out.shape, out.dtype) for out in outs],
        in_specs=[hbm] * 3,
        out_specs=[pl.BlockSpec(memory_space=pltpu.HBM)] * 3,
        scratch_shapes=[vm(out.shape, F32) for out in outs] + [dma((6,))],
        compiler_params=pltpu.CompilerParams(vmem_limit_bytes=63 * 2**20),
    )(*outs))


def solution(mesh):
    in_specs = (P("dy", "dx", None), P("dy", "dx"), P("dy", "dx", None, None), P(), P(), P(), P())
    out_specs = (P(), P(), P("dy", None))
    return jax.shard_map(
        on_device, mesh=mesh, in_specs=in_specs, out_specs=out_specs, check_vma=False
    )
```
